128 devices in a mesh: row: 8 (over y, z_hi), col: 16 (over z_lo, x, core).
Axes of the slice: x: 4, y: 4, z: 4 (z_hi: 2, z_lo: 2; z = z_hi * 2 + z_lo), core: 2. Of those that a mesh axis runs over, the one named last changes fastest.
Arguments:
- pair_rows: float32 [768, 768, 128], P(('row', 'col')), may hold values from -6 to 6
- valid_count: int32 [1], replicated, may hold values from 384 to 767
- start_proj: float32 [4, 128, 128], replicated, may hold values from -0.9 to 0.9
- start_out: float32 [128, 128], replicated, may hold values from -0.72 to 0.72
- start_bias: float32 [128, 4], replicated, may hold values from -1.08 to 1.08
- end_proj: float32 [4, 128, 128], replicated, may hold values from -0.9 to 0.9
- end_out: float32 [128, 128], replicated, may hold values from -0.72 to 0.72
- end_bias: float32 [128, 4], replicated, may hold values from -1.08 to 1.08
Outputs:
- pair_out: float32 [768, 768, 128], P(('row', 'col'))
The draws below stay inside these ranges and needn't reach their ends.
All inputs are finite; a program needn't handle non-finite values.
Results may differ from the reference program's by a relative error of at most 0.00007.
Values sent between devices are 32-bit elements; how exact they have to be, the bound alone decides.
No kernel may reach another device: no remote copies, remote signals or barrier semaphores. Data moves between devices by JAX's collectives and lax.ppermute only.
A program may use at most 128 MiB of HBM per device.

```python
import jax
import jax.numpy as jnp
from jax import lax

H = 4
C = 128
N = 768


def steps_of(rng, shape, shards, least, high):
    loudness, own = 1.0, jax.random.fold_in(rng, 6)
    for dim, parts in shards:
        steps = jnp.exp(jax.random.uniform(jax.random.fold_in(own, dim), (parts,), jnp.float32, least / len(shards), high / len(shards)))
        loudness = loudness * jnp.repeat(steps, shape[dim] // parts).reshape([-1 if axis == dim else 1 for axis in range(len(shape))])
    return loudness


def scatter_about(stream_key, dims, deviation, reach, cuts=(), kind=jnp.bfloat16):
    result = jax.random.normal(stream_key, dims, jnp.float32) * deviation
    if len(cuts) > 0:
        result = steps_of(stream_key, dims, cuts, -0.22, 0.18) * result
    return jnp.clip(result, min=-reach, max=reach).astype(kind)


def setup_inputs(seed: int = 0) -> dict:
    seeds = jax.random.split(jax.random.key(seed), 9)
    return {
        "pair_rows": scatter_about(seeds[0], (N, N, C), 1.0, 6.0, ((0, 128),), jnp.float32),
        "valid_count": jax.random.randint(seeds[1], (1,), N // 2, N).astype(jnp.int32),
        "start_proj": scatter_about(seeds[2], (4, C, C), 0.15, 0.9, (), jnp.float32),
        "start_out": scatter_about(seeds[3], (C, C), 0.12, 0.72, (), jnp.float32),
        "start_bias": scatter_about(seeds[4], (C, H), 0.18, 1.08, (), jnp.float32),
        "end_proj": scatter_about(seeds[5], (4, C, C), 0.15, 0.9, (), jnp.float32),
        "end_out": scatter_about(seeds[6], (C, C), 0.12, 0.72, (), jnp.float32),
        "end_bias": scatter_about(seeds[7], (C, H), 0.18, 1.08, (), jnp.float32),
    }


HIGHEST = lax.Precision.HIGHEST
MASKED = -1000000000.0

def layer_norm(values):
    average = lax.optimization_barrier(jnp.mean(values, axis=-1, keepdims=True))
    centred = values - average
    variance = lax.optimization_barrier(jnp.mean(centred * centred, axis=-1, keepdims=True))
    return centred * lax.rsqrt(variance + 1e-05)

def attend_row(query_row, key_row, value_row, bias_block, key_keep, head_count):
    query_count = query_row.shape[0]
    key_count = key_row.shape[0]
    head_size = query_row.shape[1] // head_count
    query_heads = query_row.reshape(query_count, head_count, head_size)
    key_heads = key_row.reshape(key_count, head_count, head_size)
    value_heads = value_row.reshape(key_count, head_count, head_size)
    scores = jnp.einsum('jhd,khd->hjk', query_heads, key_heads, precision=HIGHEST) + bias_block
    scores = jnp.where(key_keep[None, None, :], scores, MASKED)
    weights = jnp.exp(scores)
    totals = lax.optimization_barrier(jnp.sum(weights, axis=2))
    mixed = jnp.einsum('hjk,khd->jhd', weights, value_heads, precision=HIGHEST) / jnp.transpose(totals)[:, :, None]
    return mixed.reshape(query_count, head_count * head_size)

def triangle(grid, projection, out_weight, bias_weight, key_keep):
    head_count = bias_weight.shape[1]
    q_scale = (grid.shape[2] // head_count) ** (-0.5)
    normed = layer_norm(grid)
    bias_full = jnp.einsum('jkc,ch->hjk', normed, bias_weight, precision=HIGHEST)

    def one_row(row_values):
        stacked = jnp.einsum('nc,pcd->pnd', row_values, projection, precision=HIGHEST)
        mixed = attend_row(stacked[0] * q_scale, stacked[1], stacked[2], bias_full, key_keep, head_count)
        gated = mixed * jax.nn.sigmoid(stacked[3])
        return jnp.dot(gated, out_weight, precision=HIGHEST)
    return lax.map(one_row, normed)

def reference(pair_rows, valid_count, start_proj, start_out, start_bias, end_proj, end_out, end_bias):
    length = pair_rows.shape[0]
    key_keep = jnp.arange(length, dtype=jnp.int32) < valid_count[0]
    updated = pair_rows + triangle(pair_rows, start_proj, start_out, start_bias, key_keep)
    turned = jnp.swapaxes(updated, 0, 1)
    return turned + triangle(turned, end_proj, end_out, end_bias, key_keep)
```

```python
import functools
import jax
import jax.numpy as jnp
from jax import lax
from jax.sharding import PartitionSpec as P
from jax.experimental import pallas as pl
from jax.experimental.pallas import tpu as pltpu

LOG2E = 1.4426950408889634
BF = jnp.bfloat16
F32 = jnp.float32
HIGHEST = lax.Precision.HIGHEST
ROWS, N, C, H, D = 6, 768, 128, 4, 32


def normalise(values):
    average = jnp.mean(values, axis=-1, keepdims=True)
    centred = values - average
    variance = jnp.mean(centred * centred, axis=-1, keepdims=True)
    return centred * lax.rsqrt(variance + 1e-05)


def halves(values):
    high = values.astype(BF)
    return high, (values - high.astype(F32)).astype(BF)


def bias_kernel(z_ref, weight_ref, bias_ref):
    u = normalise(z_ref[0])
    b = lax.dot_general(
        weight_ref[...], u, (((1,), (1,)), ((), ())), precision=HIGHEST, preferred_element_type=F32
    )
    for block in range(N // 128):
        bias_ref[0, block * H : (block + 1) * H, :] = b[:H, block * 128 : (block + 1) * 128]


def bias_call(z, bias_weight):
    rows = z.shape[0]
    weight = jnp.pad(bias_weight.T * LOG2E, ((0, 8 - H), (0, 0)))
    return pl.pallas_call(
        bias_kernel,
        grid=(rows,),
        in_specs=[
            pl.BlockSpec((1, N, C), lambda r: (r, 0, 0)),
            pl.BlockSpec((8, C), lambda r: (0, 0)),
        ],
        out_specs=pl.BlockSpec((1, N // 128 * H, 128), lambda r: (r, 0, 0)),
        out_shape=jax.ShapeDtypeStruct((rows, N // 128 * H, 128), F32),
        cost_estimate=pl.CostEstimate(flops=rows * N * C * 20, bytes_accessed=rows * N * C * 4, transcendentals=0),
        name="bias",
    )(z, weight)


def project_kernel(valid_ref, z_ref, p_ref, q_ref, k_ref, v_ref, g_ref, w_ref, wg_ref):
    lane = lax.broadcasted_iota(jnp.int32, (1, C), 1)
    group = lane // D

    @pl.when(pl.program_id(0) == 0)
    def _():
        group_c = lax.broadcasted_iota(jnp.int32, (C, C), 1) // D
        for part in range(3):
            base = p_ref[part]
            if part == 0:
                base = base * (LOG2E * D**-0.5)
            turned = [base] + [pltpu.roll(base, D * m, 1) for m in range(1, 4)]
            for head in range(H):
                block = turned[(0 - head) % H]
                for g in range(1, H):
                    block = jnp.where(group_c == g, turned[(g - head) % H], block)
                high, low = halves(block)
                at = pl.ds((part * H + head) * C, C)
                w_ref[0, :C, at] = high
                w_ref[0, C:, at] = high
                w_ref[1, :C, at] = low
                w_ref[1, C:, at] = low
        high, low = halves(p_ref[3])
        wg_ref[0, :C] = high
        wg_ref[0, C:] = high
        wg_ref[1, :C] = low
        wg_ref[1, C:] = low

    u = normalise(z_ref[0])
    u_high, u_low = halves(u)
    u2 = jnp.concatenate([u_high, u_low], axis=1)

    def project(w):
        return jnp.dot(u2, w[0], preferred_element_type=F32) + jnp.dot(
            u2, w[1], preferred_element_type=F32
        )

    dead = lax.broadcasted_iota(jnp.int32, (N, 1), 0) >= valid_ref[0]
    dead_value = jnp.where(dead, -1e9, 0.0)
    for part in range(3):
        for head in range(H):
            at = pl.ds((part * H + head) * C, C)
            x = project((w_ref[0, :, at], w_ref[1, :, at]))
            high = x.astype(BF).astype(F32)
            low = x - high
            if part == 0:
                out = jnp.where(group == 1, low, high)
                out = jnp.where(group == 3, jnp.where(lane == 3 * D, 1.0, 0.0), out)
                q_ref[0, head] = out.astype(BF)
            elif part == 1:
                out = jnp.where(group == 2, low, high)
                out = jnp.where(group == 3, jnp.where(lane == 3 * D, dead_value, 0.0), out)
                k_ref[0, head] = out.astype(BF)
            else:
                out = jnp.where(group == (head + 1) % H, low, high)
                out = jnp.where(group == (head + 2) % H, 1.0, out)
                out = jnp.where(group == (head + 3) % H, 0.0, out)
                v_ref[0, head] = out.astype(BF)
    g_ref[0] = jax.nn.sigmoid(project((wg_ref[0], wg_ref[1])))


def project_call(z, projection, valid_count):
    rows = z.shape[0]
    heads = jax.ShapeDtypeStruct((rows, H, N, C), BF)
    head_spec = pl.BlockSpec((1, H, N, C), lambda r, s: (r, 0, 0, 0))
    row_spec = pl.BlockSpec((1, N, C), lambda r, s: (r, 0, 0))
    return pl.pallas_call(
        project_kernel,
        grid_spec=pltpu.PrefetchScalarGridSpec(
            num_scalar_prefetch=1,
            grid=(rows,),
            in_specs=[row_spec, pl.BlockSpec((4, C, C), lambda r, s: (0, 0, 0))],
            out_specs=[head_spec, head_spec, head_spec, row_spec],
            scratch_shapes=[
                pltpu.VMEM((2, 2 * C, 3 * H * C), BF),
                pltpu.VMEM((2, 2 * C, C), BF),
            ],
        ),
        out_shape=[heads, heads, heads, jax.ShapeDtypeStruct((rows, N, C), F32)],
        compiler_params=pltpu.CompilerParams(vmem_limit_bytes=50 * 2**20),
        cost_estimate=pl.CostEstimate(
            flops=rows * N * 2 * C * 2 * 13 * C * 2, bytes_accessed=rows * N * C * 4 * 8, transcendentals=0
        ),
        name="project",
    )(valid_count, z, projection)


def attend_kernel(QC, KT, valid_ref, q_ref, k_ref, v_ref, g_ref, z_ref, bias_ref, o_ref, out_ref,
                  bias_s, acc_s, o_s):
    lane = lax.broadcasted_iota(jnp.int32, (1, C), 1)
    group = lane // D

    @pl.when((pl.program_id(0) == 0) & (pl.program_id(1) == 0))
    def _():
        high, low = halves(o_ref[...])
        o_s[0, :C] = high
        o_s[0, C:] = high
        o_s[1, :C] = low
        o_s[1, C:] = low

    @pl.when(pl.program_id(1) == 0)
    def _():
        for block in range(N // 128):
            for head in range(H):
                bias_s[head, :, block * 128 : (block + 1) * 128] = bias_ref[
                    pl.ds(block * H + head, QC, stride=N // 128 * H), :
                ]

    def run(keys):
        for head in range(H):
            q = q_ref[0, head]
            acc = None
            for at in range(0, keys, KT):
                size = min(KT, keys - at)
                s = lax.dot_general(
                    q, k_ref[0, head, at : at + size, :], (((1,), (1,)), ((), ())),
                    preferred_element_type=F32,
                )
                w = jnp.exp2(s + bias_s[head, :, at : at + size])
                high, low = halves(w)
                v = v_ref[0, head, at : at + size, :]
                term = jnp.dot(high, v, preferred_element_type=F32) + jnp.dot(
                    low, v, preferred_element_type=F32
                )
                acc = term if acc is None else acc + term
            acc_s[head] = acc

    count = (valid_ref[0] + 127) // 128
    for blocks in range(3, N // 128 + 1):

        @pl.when(count == blocks)
        def _():
            run(blocks * 128)

    mixed = None
    for head in range(H):
        acc = acc_s[head]
        total = pltpu.roll(acc, 2 * D, 1)
        value = (acc + pltpu.roll(acc, 3 * D, 1)) / jnp.where(group == head, total, 1.0)
        mixed = value if mixed is None else jnp.where(group == head, value, mixed)
    high, low = halves(mixed * g_ref[0])
    both = jnp.concatenate([high, low], axis=1)
    out_ref[0] = (
        z_ref[0]
        + jnp.dot(both, o_s[0], preferred_element_type=F32)
        + jnp.dot(both, o_s[1], preferred_element_type=F32)
    )


def attend_call(q, k, v, g, z, bias, out_weight, valid_count, QC=256, KT=256):
    rows = z.shape[0]
    queries = z.shape[1]
    per = N // 128 * H
    key_spec = pl.BlockSpec((1, H, N, C), lambda c, r, s: (r, 0, 0, 0))
    row_spec = pl.BlockSpec((1, QC, C), lambda c, r, s: (r, c, 0))
    return pl.pallas_call(
        functools.partial(attend_kernel, QC, KT),
        grid_spec=pltpu.PrefetchScalarGridSpec(
            num_scalar_prefetch=1,
            grid=(queries // QC, rows),
            in_specs=[
                pl.BlockSpec((1, H, QC, C), lambda c, r, s: (r, 0, c, 0)),
                key_spec,
                key_spec,
                row_spec,
                row_spec,
                pl.BlockSpec((QC * per, 128), lambda c, r, s: (c, 0)),
                pl.BlockSpec((C, C), lambda c, r, s: (0, 0)),
            ],
            out_specs=row_spec,
            scratch_shapes=[
                pltpu.VMEM((H, QC, N), F32),
                pltpu.VMEM((H, QC, C), F32),
                pltpu.VMEM((2, 2 * C, C), BF),
            ],
        ),
        out_shape=jax.ShapeDtypeStruct(z.shape, F32),
        compiler_params=pltpu.CompilerParams(vmem_limit_bytes=50 * 2**20),
        cost_estimate=pl.CostEstimate(
            flops=rows * queries * N * H * 64 * 4, bytes_accessed=rows * N * C * 4 * 8, transcendentals=0
        ),
        name="attend",
    )(valid_count, q, k, v, g, z, bias, out_weight)


def per_device(
    pair_rows, valid_count, start_proj, start_out, start_bias, end_proj, end_out, end_bias
):
    axes = ("row", "col")

    def block(z, projection, out_weight, bias_weight):
        local = bias_call(z, bias_weight).reshape(-1, 128)
        bias = lax.all_gather(local, axes, axis=0, tiled=True)
        q, k, v, g = project_call(z, projection, valid_count)
        return attend_call(q, k, v, g, z, bias, out_weight, valid_count)

    updated = block(pair_rows, start_proj, start_out, start_bias)
    columns = lax.all_to_all(updated, axes, split_axis=1, concat_axis=0, tiled=True)
    turned = jnp.swapaxes(columns, 0, 1)
    return block(turned, end_proj, end_out, end_bias)


def solution(mesh):
    return jax.shard_map(
        per_device,
        mesh=mesh,
        in_specs=(P(("row", "col"), None, None), P(), P(), P(), P(), P(), P(), P()),
        out_specs=P(("row", "col"), None, None),
        check_vma=False,
    )
```

```python
import functools
import jax
import jax.numpy as jnp
from jax import lax
from jax.sharding import PartitionSpec as P
from jax.experimental import pallas as pl
from jax.experimental.pallas import tpu as pltpu

LOG2E = 1.4426950408889634
BF = jnp.bfloat16
F32 = jnp.float32
HIGHEST = lax.Precision.HIGHEST
ROWS, N, C, H, D = 6, 768, 128, 4, 32


def normalise(values):
    average = jnp.mean(values, axis=-1, keepdims=True)
    centred = values - average
    variance = jnp.mean(centred * centred, axis=-1, keepdims=True)
    return centred * lax.rsqrt(variance + 1e-05)


def halves(values):
    high = values.astype(BF)
    return high, (values - high.astype(F32)).astype(BF)


def bias_kernel(z_ref, weight_ref, bias_ref):
    u = normalise(z_ref[0])
    b = lax.dot_general(
        weight_ref[...], u, (((1,), (1,)), ((), ())), precision=HIGHEST, preferred_element_type=F32
    )
    for block in range(N // 128):
        bias_ref[0, block * H : (block + 1) * H, :] = b[:H, block * 128 : (block + 1) * 128]


def bias_call(z, bias_weight):
    rows = z.shape[0]
    weight = jnp.pad(bias_weight.T * LOG2E, ((0, 8 - H), (0, 0)))
    return pl.pallas_call(
        bias_kernel,
        grid=(rows,),
        in_specs=[
            pl.BlockSpec((1, N, C), lambda r: (r, 0, 0)),
            pl.BlockSpec((8, C), lambda r: (0, 0)),
        ],
        out_specs=pl.BlockSpec((1, N // 128 * H, 128), lambda r: (r, 0, 0)),
        out_shape=jax.ShapeDtypeStruct((rows, N // 128 * H, 128), F32),
        cost_estimate=pl.CostEstimate(flops=rows * N * C * 20, bytes_accessed=rows * N * C * 4, transcendentals=0),
        name="bias",
    )(z, weight)


def project_kernel(valid_ref, z_ref, p_ref, q_ref, k_ref, v_ref, g_ref, w_ref, wg_ref):
    lane = lax.broadcasted_iota(jnp.int32, (1, C), 1)
    group = lane // D

    @pl.when(pl.program_id(0) == 0)
    def _():
        group_c = lax.broadcasted_iota(jnp.int32, (C, C), 1) // D
        for part in range(3):
            base = p_ref[part]
            if part == 0:
                base = base * (LOG2E * D**-0.5)
            turned = [base] + [pltpu.roll(base, D * m, 1) for m in range(1, 4)]
            for head in range(H):
                block = turned[(0 - head) % H]
                for g in range(1, H):
                    block = jnp.where(group_c == g, turned[(g - head) % H], block)
                high, low = halves(block)
                at = pl.ds((part * H + head) * C, C)
                w_ref[0, :C, at] = high
                w_ref[0, C:, at] = high
                w_ref[1, :C, at] = low
                w_ref[1, C:, at] = low
        high, low = halves(p_ref[3])
        wg_ref[0, :C] = high
        wg_ref[0, C:] = high
        wg_ref[1, :C] = low
        wg_ref[1, C:] = low

    u = normalise(z_ref[0])
    u_high, u_low = halves(u)
    u2 = jnp.concatenate([u_high, u_low], axis=1)

    def project(w):
        return jnp.dot(u2, w[0], preferred_element_type=F32) + jnp.dot(
            u2, w[1], preferred_element_type=F32
        )

    dead = lax.broadcasted_iota(jnp.int32, (N, 1), 0) >= valid_ref[0]
    dead_value = jnp.where(dead, -1e9, 0.0)
    for part in range(3):
        for head in range(H):
            at = pl.ds((part * H + head) * C, C)
            x = project((w_ref[0, :, at], w_ref[1, :, at]))
            high = x.astype(BF).astype(F32)
            low = x - high
            if part == 0:
                out = jnp.where(group == 1, low, high)
                out = jnp.where(group == 3, jnp.where(lane == 3 * D, 1.0, 0.0), out)
                q_ref[0, head] = out.astype(BF)
            elif part == 1:
                out = jnp.where(group == 2, low, high)
                out = jnp.where(group == 3, jnp.where(lane == 3 * D, dead_value, 0.0), out)
                k_ref[0, head] = out.astype(BF)
            else:
                out = jnp.where(group == (head + 1) % H, low, high)
                out = jnp.where(group == (head + 2) % H, 1.0, out)
                out = jnp.where(group == (head + 3) % H, 0.0, out)
                v_ref[0, head] = out.astype(BF)
    g_ref[0] = jax.nn.sigmoid(project((wg_ref[0], wg_ref[1])))


def project_call(z, projection, valid_count):
    rows = z.shape[0]
    heads = jax.ShapeDtypeStruct((rows, H, N, C), BF)
    head_spec = pl.BlockSpec((1, H, N, C), lambda r, s: (r, 0, 0, 0))
    row_spec = pl.BlockSpec((1, N, C), lambda r, s: (r, 0, 0))
    return pl.pallas_call(
        project_kernel,
        grid_spec=pltpu.PrefetchScalarGridSpec(
            num_scalar_prefetch=1,
            grid=(rows,),
            in_specs=[row_spec, pl.BlockSpec((4, C, C), lambda r, s: (0, 0, 0))],
            out_specs=[head_spec, head_spec, head_spec, row_spec],
            scratch_shapes=[
                pltpu.VMEM((2, 2 * C, 3 * H * C), BF),
                pltpu.VMEM((2, 2 * C, C), BF),
            ],
        ),
        out_shape=[heads, heads, heads, jax.ShapeDtypeStruct((rows, N, C), F32)],
        compiler_params=pltpu.CompilerParams(vmem_limit_bytes=50 * 2**20),
        cost_estimate=pl.CostEstimate(
            flops=rows * N * 2 * C * 2 * 13 * C * 2, bytes_accessed=rows * N * C * 4 * 8, transcendentals=0
        ),
        name="project",
    )(valid_count, z, projection)


def attend_kernel(rows, QC, KT, transposed, valid_ref, q_ref, k_ref, v_ref, g_ref, z_ref, bias_ref, o_ref,
                  out_ref, bias_s, acc_s, o_s):
    group = lax.broadcasted_iota(jnp.int32, (1, C), 1) // D
    chunk, row = pl.program_id(0), pl.program_id(1)
    per = N // 128 * H

    @pl.when((chunk == 0) & (row == 0))
    def _():
        high, low = halves(o_ref[...])
        o_s[0, :C] = high
        o_s[0, C:] = high
        o_s[1, :C] = low
        o_s[1, C:] = low

    @pl.when(row == 0)
    def _():
        for head in range(H):
            for block in range(N // 128):
                at = pl.ds(block * 128, 128)
                if transposed:
                    for part in range(QC // 128):
                        first = block * 128 * per + (chunk * (QC // 128) + part) * H + head
                        tile = bias_ref[pl.ds(first, 128, stride=per), :]
                        bias_s[head, pl.ds(part * 128, 128), at] = tile.T
                else:
                    bias_s[head, :, at] = bias_ref[pl.ds(block * H + head, QC, stride=per), :]

    def finish():
        slot = (row + 1) % 2
        value = low_value = total = None
        for head in range(H):
            acc = acc_s[slot, head]
            if head == 0:
                value = low_value = total = acc
            else:
                value = jnp.where(group == head, acc, value)
                low_value = jnp.where(group == (head + 1) % H, acc, low_value)
                total = jnp.where(group == (head + 2) % H, acc, total)
        value = value + pltpu.roll(low_value, 3 * D, 1)
        mixed = value / pltpu.roll(total, 2 * D, 1) * g_ref[0]
        high, low = halves(mixed)
        both = jnp.concatenate([high, low], axis=1)
        out_ref[0] = (
            z_ref[0]
            + jnp.dot(both, o_s[0], preferred_element_type=F32)
            + jnp.dot(both, o_s[1], preferred_element_type=F32)
        )

    def run(keys):
        for head in range(H):
            q = q_ref[0, head]
            acc = None
            for at in range(0, keys, KT):
                size = min(KT, keys - at)
                s = lax.dot_general(
                    q, k_ref[0, head, at : at + size, :], (((1,), (1,)), ((), ())),
                    preferred_element_type=F32,
                )
                w = jnp.exp2(s + bias_s[head, :, at : at + size])
                high, low = halves(w)
                v = v_ref[0, head, at : at + size, :]
                term = jnp.dot(high, v, preferred_element_type=F32) + jnp.dot(
                    low, v, preferred_element_type=F32
                )
                acc = term if acc is None else acc + term
            acc_s[row % 2, head] = acc

    count = (valid_ref[0] + 127) // 128
    for blocks in range(3, N // 128 + 1):

        @pl.when((count == blocks) & (row < rows))
        def _():
            run(blocks * 128)
            finish()

    @pl.when(row == rows)
    def _():
        finish()


def attend_call(q, k, v, g, z, bias, out_weight, valid_count, QC=384, KT=256, transposed=False):
    rows = z.shape[0]
    queries = z.shape[1]
    per = N // 128 * H
    now = lambda r: jnp.minimum(r, rows - 1)
    last = lambda r: jnp.maximum(r - 1, 0)
    key_spec = pl.BlockSpec((1, H, N, C), lambda c, r, s: (now(r), 0, 0, 0))
    row_spec = pl.BlockSpec((1, QC, C), lambda c, r, s: (last(r), c, 0))
    if transposed:
        bias_spec = pl.BlockSpec((N * per, 128), lambda c, r, s: (0, 0))
    else:
        bias_spec = pl.BlockSpec((QC * per, 128), lambda c, r, s: (c, 0))
    return pl.pallas_call(
        functools.partial(attend_kernel, rows, QC, KT, transposed),
        grid_spec=pltpu.PrefetchScalarGridSpec(
            num_scalar_prefetch=1,
            grid=(queries // QC, rows + 1),
            in_specs=[
                pl.BlockSpec((1, H, QC, C), lambda c, r, s: (now(r), 0, c, 0)),
                key_spec,
                key_spec,
                row_spec,
                row_spec,
                bias_spec,
                pl.BlockSpec((C, C), lambda c, r, s: (0, 0)),
            ],
            out_specs=row_spec,
            scratch_shapes=[
                pltpu.VMEM((H, QC, N), F32),
                pltpu.VMEM((2, H, QC, C), F32),
                pltpu.VMEM((2, 2 * C, C), BF),
            ],
        ),
        out_shape=jax.ShapeDtypeStruct(z.shape, F32),
        compiler_params=pltpu.CompilerParams(vmem_limit_bytes=56 * 2**20),
        cost_estimate=pl.CostEstimate(
            flops=rows * queries * N * H * 64 * 4, bytes_accessed=rows * N * C * 4 * 8, transcendentals=0
        ),
        name="attend",
    )(valid_count, q, k, v, g, z, bias, out_weight)


def per_device(
    pair_rows, valid_count, start_proj, start_out, start_bias, end_proj, end_out, end_bias
):
    axes = ("row", "col")

    def gather_bias(z, bias_weight):
        return lax.all_gather(bias_call(z, bias_weight).reshape(-1, 128), axes, axis=0, tiled=True)

    start_gathered = gather_bias(pair_rows, start_bias)
    q, k, v, g = project_call(pair_rows, start_proj, valid_count)
    updated = attend_call(q, k, v, g, pair_rows, start_gathered, start_out, valid_count, N)
    end_gathered = gather_bias(updated, end_bias)
    columns = lax.all_to_all(updated, axes, split_axis=1, concat_axis=0, tiled=True)
    turned = jnp.swapaxes(columns, 0, 1)
    q, k, v, g = project_call(turned, end_proj, valid_count)
    return attend_call(q, k, v, g, turned, end_gathered, end_out, valid_count, N, transposed=True)


def solution(mesh):
    return jax.shard_map(
        per_device,
        mesh=mesh,
        in_specs=(P(("row", "col"), None, None), P(), P(), P(), P(), P(), P(), P()),
        out_specs=P(("row", "col"), None, None),
        check_vma=False,
    )
```

```python
import functools
import jax
import jax.numpy as jnp
from jax import lax
from jax.sharding import Mesh, PartitionSpec as P
from jax.experimental import pallas as pl
from jax.experimental.pallas import tpu as pltpu

LOG2E = 1.4426950408889634
BF = jnp.bfloat16
F32 = jnp.float32
HIGHEST = lax.Precision.HIGHEST
AXES = ("y", "z_hi", "z_lo", "x", "core")
ROWS, N, C, H, D = 6, 768, 128, 4, 32


def normalise(values):
    average = jnp.mean(values, axis=-1, keepdims=True)
    centred = values - average
    variance = jnp.mean(centred * centred, axis=-1, keepdims=True)
    return centred * lax.rsqrt(variance + 1e-05)


def halves(values):
    high = values.astype(BF)
    return high, (values - high.astype(F32)).astype(BF)


def bias_kernel(z_ref, weight_ref, bias_ref):
    u = normalise(z_ref[0])
    b = lax.dot_general(
        weight_ref[...], u, (((1,), (1,)), ((), ())), precision=HIGHEST, preferred_element_type=F32
    )
    for block in range(N // 128):
        bias_ref[0, block * H : (block + 1) * H, :] = b[:H, block * 128 : (block + 1) * 128]


def bias_call(z, bias_weight):
    rows = z.shape[0]
    weight = jnp.pad(bias_weight.T * LOG2E, ((0, 8 - H), (0, 0)))
    return pl.pallas_call(
        bias_kernel,
        grid=(rows,),
        in_specs=[
            pl.BlockSpec((1, N, C), lambda r: (r, 0, 0)),
            pl.BlockSpec((8, C), lambda r: (0, 0)),
        ],
        out_specs=pl.BlockSpec((1, N // 128 * H, 128), lambda r: (r, 0, 0)),
        out_shape=jax.ShapeDtypeStruct((rows, N // 128 * H, 128), F32),
        cost_estimate=pl.CostEstimate(flops=rows * N * C * 20, bytes_accessed=rows * N * C * 4, transcendentals=0),
        name="bias",
    )(z, weight)


def split_bias_kernel(pos_ref, z_ref, weight_ref, keep_ref, send_ref):
    u = normalise(z_ref[...].reshape(2 * N, C))
    b = lax.dot_general(
        weight_ref[...], u, (((1,), (1,)), ((), ())), precision=HIGHEST, preferred_element_type=F32
    )
    first = pos_ref[3] == 0
    for row in range(2):
        for block in range(3):
            at = row * N + block * 128
            low = b[:H, at : at + 128]
            high = b[:H, at + 384 : at + 512]
            to = pl.ds(row * 12 + block * H, H)
            keep_ref[to, :] = jnp.where(first, low, high)
            send_ref[to, :] = jnp.where(first, high, low)


def split_bias_call(z, bias_weight, pos):
    rows = z.shape[0]
    weight = jnp.pad(bias_weight.T * LOG2E, ((0, 8 - H), (0, 0)))
    out = jax.ShapeDtypeStruct((rows * 12, 128), F32)
    out_spec = pl.BlockSpec((24, 128), lambda r, s: (r, 0))
    return pl.pallas_call(
        split_bias_kernel,
        grid_spec=pltpu.PrefetchScalarGridSpec(
            num_scalar_prefetch=1,
            grid=(rows // 2,),
            in_specs=[
                pl.BlockSpec((2, N, C), lambda r, s: (r, 0, 0)),
                pl.BlockSpec((8, C), lambda r, s: (0, 0)),
            ],
            out_specs=[out_spec, out_spec],
        ),
        out_shape=[out, out],
        cost_estimate=pl.CostEstimate(flops=rows * N * C * 20, bytes_accessed=rows * N * C * 4, transcendentals=0),
        name="bias",
    )(pos, z, weight)


OFFSETS = (0, 3, 1, 2)


def device_index(y, z, x, core):
    return ((y % 4) * 4 + z % 4) * 8 + (x % 4) * 2 + core


def moves(first, second, step):
    pairs = []
    for y in range(4):
        for z in range(4):
            for x in range(4):
                for core in range(2):
                    axis = (first, second)[core]
                    to = (y + step * (axis == "y"), z + step * (axis == "z"), x + step * (axis == "x"))
                    pairs.append((device_index(y, z, x, core), device_index(*to, core)))
    return pairs


SWAP = [(d, d ^ 1) for d in range(128)]


def ring_gather(keep, send, x, core):
    def move(value, pairs):
        return lax.ppermute(value, AXES, pairs)

    other = move(send, SWAP)
    chip = jnp.where(core == 0, jnp.concatenate([keep, other]), jnp.concatenate([other, keep]))
    before = move(chip, moves("x", "x", 1))
    after = move(chip, moves("x", "x", -1))
    across = move(chip, moves("x", "x", 2))
    size = chip.shape[0]
    line = jnp.concatenate([chip, after, across, before] * 2)
    block = lax.dynamic_slice_in_dim(line, ((4 - x) % 4) * size, 4 * size)

    def along(block, first, second):
        half = block.shape[0] // 2
        up, down = moves(first, second, 1), moves(first, second, -1)
        before, after = move(block, up), move(block, down)
        return [block, before, after, move(before[:half], up), move(after[half:], down)]

    plane = jnp.concatenate(along(block, "z", "y"))
    own = along(plane, "y", "z")
    return own + [move(piece, SWAP) for piece in own]


def project_kernel(valid_ref, z_ref, p_ref, q_ref, k_ref, v_ref, g_ref, w_ref, wg_ref):
    lane = lax.broadcasted_iota(jnp.int32, (1, C), 1)
    group = lane // D

    @pl.when(pl.program_id(0) == 0)
    def _():
        group_c = lax.broadcasted_iota(jnp.int32, (C, C), 1) // D
        for part in range(3):
            base = p_ref[part]
            if part == 0:
                base = base * (LOG2E * D**-0.5)
            turned = [base] + [pltpu.roll(base, D * m, 1) for m in range(1, 4)]
            for head in range(H):
                block = turned[(0 - head) % H]
                for g in range(1, H):
                    block = jnp.where(group_c == g, turned[(g - head) % H], block)
                high, low = halves(block)
                at = pl.ds((part * H + head) * C, C)
                w_ref[0, :C, at] = high
                w_ref[0, C:, at] = high
                w_ref[1, :C, at] = low
                w_ref[1, C:, at] = low
        high, low = halves(p_ref[3])
        wg_ref[0, :C] = high
        wg_ref[0, C:] = high
        wg_ref[1, :C] = low
        wg_ref[1, C:] = low

    u = normalise(z_ref[0])
    u_high, u_low = halves(u)
    u2 = jnp.concatenate([u_high, u_low], axis=1)

    def project(w):
        return jnp.dot(u2, w[0], preferred_element_type=F32) + jnp.dot(
            u2, w[1], preferred_element_type=F32
        )

    dead = lax.broadcasted_iota(jnp.int32, (N, 1), 0) >= valid_ref[0]
    dead_value = jnp.where(dead, -1e9, 0.0)
    for part in range(3):
        for head in range(H):
            at = pl.ds((part * H + head) * C, C)
            x = project((w_ref[0, :, at], w_ref[1, :, at]))
            high = x.astype(BF).astype(F32)
            low = x - high
            if part == 0:
                out = jnp.where(group == 1, low, high)
                out = jnp.where(group == 3, jnp.where(lane == 3 * D, 1.0, 0.0), out)
                q_ref[0, head] = out.astype(BF)
            elif part == 1:
                out = jnp.where(group == 2, low, high)
                out = jnp.where(group == 3, jnp.where(lane == 3 * D, dead_value, 0.0), out)
                k_ref[0, head] = out.astype(BF)
            else:
                out = jnp.where(group == (head + 1) % H, low, high)
                out = jnp.where(group == (head + 2) % H, 1.0, out)
                out = jnp.where(group == (head + 3) % H, 0.0, out)
                v_ref[0, head] = out.astype(BF)
    g_ref[0] = jax.nn.sigmoid(project((wg_ref[0], wg_ref[1])))


def project_call(z, projection, valid_count):
    rows = z.shape[0]
    heads = jax.ShapeDtypeStruct((rows, H, N, C), BF)
    head_spec = pl.BlockSpec((1, H, N, C), lambda r, s: (r, 0, 0, 0))
    row_spec = pl.BlockSpec((1, N, C), lambda r, s: (r, 0, 0))
    return pl.pallas_call(
        project_kernel,
        grid_spec=pltpu.PrefetchScalarGridSpec(
            num_scalar_prefetch=1,
            grid=(rows,),
            in_specs=[row_spec, pl.BlockSpec((4, C, C), lambda r, s: (0, 0, 0))],
            out_specs=[head_spec, head_spec, head_spec, row_spec],
            scratch_shapes=[
                pltpu.VMEM((2, 2 * C, 3 * H * C), BF),
                pltpu.VMEM((2, 2 * C, C), BF),
            ],
        ),
        out_shape=[heads, heads, heads, jax.ShapeDtypeStruct((rows, N, C), F32)],
        compiler_params=pltpu.CompilerParams(vmem_limit_bytes=50 * 2**20),
        cost_estimate=pl.CostEstimate(
            flops=rows * N * 2 * C * 2 * 13 * C * 2, bytes_accessed=rows * N * C * 4 * 8, transcendentals=0
        ),
        name="project",
    )(valid_count, z, projection)


def attend_kernel(rows, QC, KT, transposed, valid_ref, q_ref, k_ref, v_ref, g_ref, z_ref, o_ref, *refs):
    *bias_refs, out_ref, bias_s, acc_s, o_s = refs
    group = lax.broadcasted_iota(jnp.int32, (1, C), 1) // D
    chunk, row = pl.program_id(0), pl.program_id(1)
    per = N // 128 * H

    @pl.when((chunk == 0) & (row == 0))
    def _():
        high, low = halves(o_ref[...])
        o_s[0, :C] = high
        o_s[0, C:] = high
        o_s[1, :C] = low
        o_s[1, C:] = low

    @pl.when(row == 0)
    def _():
        if transposed:
            bias_ref = bias_refs[0]
            for head in range(H):
                for block in range(N // 128):
                    for part in range(QC // 128):
                        first = block * 128 * per + (chunk * (QC // 128) + part) * H + head
                        tile = bias_ref[pl.ds(first, 128, stride=per), :]
                        bias_s[head, block, pl.ds(part * 128, 128), :] = tile.T
        else:
            my_y, my_z, core = valid_ref[1], valid_ref[2], valid_ref[3]
            per_half = per // 2
            size = 48 * per_half
            for side in range(2):
                half = core if side == 0 else 1 - core
                pieces = bias_refs[side * 5 : side * 5 + 5]
                for last, last_step in enumerate(OFFSETS):
                    for mid, mid_step in enumerate(OFFSETS):
                        y_step = jnp.where(half == 0, last_step, mid_step)
                        z_step = jnp.where(half == 0, mid_step, last_step)
                        to = ((my_y + y_step) % 4) * 192 + ((my_z + z_step) % 4) * 48
                        to = pl.ds(pl.multiple_of(to, 48), 48)
                        piece, place = (pieces[last], mid) if last < 3 else (pieces[3 + mid // 2], mid % 2)
                        for head in range(H):
                            for block in range(3):
                                bias_s[head, half * 3 + block, to, :] = piece[
                                    pl.ds(place * size + block * H + head, 48, stride=per_half), :
                                ]

    def bias_of(head, at, size):
        blocks = [bias_s[head, (at + b) // 128] for b in range(0, size, 128)]
        return blocks[0] if len(blocks) == 1 else jnp.concatenate(blocks, axis=1)

    def finish():
        slot = (row + 1) % 2
        value = low_value = total = None
        for head in range(H):
            acc = acc_s[slot, head]
            if head == 0:
                value = low_value = total = acc
            else:
                value = jnp.where(group == head, acc, value)
                low_value = jnp.where(group == (head + 1) % H, acc, low_value)
                total = jnp.where(group == (head + 2) % H, acc, total)
        value = value + pltpu.roll(low_value, 3 * D, 1)
        mixed = value / pltpu.roll(total, 2 * D, 1) * g_ref[0]
        high, low = halves(mixed)
        both = jnp.concatenate([high, low], axis=1)
        out_ref[0] = (
            z_ref[0]
            + jnp.dot(both, o_s[0], preferred_element_type=F32)
            + jnp.dot(both, o_s[1], preferred_element_type=F32)
        )

    def run(keys):
        for head in range(H):
            q = q_ref[0, head]
            acc = None
            for at in range(0, keys, KT):
                size = min(KT, keys - at)
                s = lax.dot_general(
                    q, k_ref[0, head, at : at + size, :], (((1,), (1,)), ((), ())),
                    preferred_element_type=F32,
                )
                w = jnp.exp2(s + bias_of(head, at, size))
                high, low = halves(w)
                v = v_ref[0, head, at : at + size, :]
                term = jnp.dot(high, v, preferred_element_type=F32) + jnp.dot(
                    low, v, preferred_element_type=F32
                )
                acc = term if acc is None else acc + term
            acc_s[row % 2, head] = acc

    count = (valid_ref[0] + 127) // 128
    for blocks in range(3, N // 128 + 1):

        @pl.when((count == blocks) & (row < rows))
        def _():
            run(blocks * 128)
            finish()

    @pl.when(row == rows)
    def _():
        finish()


def attend_call(q, k, v, g, z, bias, out_weight, pos, QC=N, KT=256, transposed=False):
    rows = z.shape[0]
    queries = z.shape[1]
    now = lambda r: jnp.minimum(r, rows - 1)
    last = lambda r: jnp.maximum(r - 1, 0)
    key_spec = pl.BlockSpec((1, H, N, C), lambda c, r, s: (now(r), 0, 0, 0))
    row_spec = pl.BlockSpec((1, QC, C), lambda c, r, s: (last(r), c, 0))
    bias_specs = [
        pl.BlockSpec(piece.shape, lambda c, r, s: (0, 0), pipeline_mode=pl.Buffered(1)) for piece in bias
    ]
    return pl.pallas_call(
        functools.partial(attend_kernel, rows, QC, KT, transposed),
        grid_spec=pltpu.PrefetchScalarGridSpec(
            num_scalar_prefetch=1,
            grid=(queries // QC, rows + 1),
            in_specs=[
                pl.BlockSpec((1, H, QC, C), lambda c, r, s: (now(r), 0, c, 0)),
                key_spec,
                key_spec,
                row_spec,
                row_spec,
                pl.BlockSpec((C, C), lambda c, r, s: (0, 0)),
                *bias_specs,
            ],
            out_specs=row_spec,
            scratch_shapes=[
                pltpu.VMEM((H, N // 128, QC, 128), F32),
                pltpu.VMEM((2, H, QC, C), F32),
                pltpu.VMEM((2, 2 * C, C), BF),
            ],
        ),
        out_shape=jax.ShapeDtypeStruct(z.shape, F32),
        compiler_params=pltpu.CompilerParams(vmem_limit_bytes=56 * 2**20),
        cost_estimate=pl.CostEstimate(
            flops=rows * queries * N * H * 64 * 4, bytes_accessed=rows * N * C * 4 * 8, transcendentals=0
        ),
        name="attend",
    )(pos, q, k, v, g, z, out_weight, *bias)


def per_device(
    pair_rows, valid_count, start_proj, start_out, start_bias, end_proj, end_out, end_bias
):
    y, x, core = lax.axis_index("y"), lax.axis_index("x"), lax.axis_index("core")
    z = lax.axis_index(("z_hi", "z_lo"))
    pos = jnp.stack([valid_count[0], y, z, core]).astype(jnp.int32)
    keep, send = split_bias_call(pair_rows, start_bias, pos)
    start_pieces = ring_gather(keep, send, x, core)
    q, k, v, g = project_call(pair_rows, start_proj, valid_count)
    updated = attend_call(q, k, v, g, pair_rows, start_pieces, start_out, pos)
    local = bias_call(updated, end_bias).reshape(-1, 128)
    end_gathered = lax.all_gather(local, AXES, axis=0, tiled=True)
    columns = lax.all_to_all(updated, AXES, split_axis=1, concat_axis=0, tiled=True)
    turned = jnp.swapaxes(columns, 0, 1)
    q, k, v, g = project_call(turned, end_proj, valid_count)
    return attend_call(q, k, v, g, turned, [end_gathered], end_out, pos, transposed=True)


def solution(mesh):
    fine = Mesh(mesh.devices.reshape(4, 2, 2, 4, 2), AXES)
    return jax.shard_map(
        per_device,
        mesh=fine,
        in_specs=(P(AXES, None, None), P(), P(), P(), P(), P(), P(), P()),
        out_specs=P(AXES, None, None),
        check_vma=False,
    )
```

```python
import functools
import jax
import jax.numpy as jnp
from jax import lax
from jax.sharding import Mesh, PartitionSpec as P
from jax.experimental import pallas as pl
from jax.experimental.pallas import tpu as pltpu

LOG2E = 1.4426950408889634
BF = jnp.bfloat16
F32 = jnp.float32
HIGHEST = lax.Precision.HIGHEST
AXES = ("y", "z_hi", "z_lo", "x", "core")
ROWS, N, C, H, D = 6, 768, 128, 4, 32


def normalise(values):
    average = jnp.mean(values, axis=-1, keepdims=True)
    centred = values - average
    variance = jnp.mean(centred * centred, axis=-1, keepdims=True)
    return centred * lax.rsqrt(variance + 1e-05)


def halves(values):
    high = values.astype(BF)
    return high, (values - high.astype(F32)).astype(BF)


def bias_rows(z_ref, weight_ref, w_s):
    @pl.when(pl.program_id(0) == 0)
    def _():
        weight = weight_ref[...] * LOG2E
        high = weight.astype(BF).astype(F32)
        padded = jnp.concatenate([high, weight - high, jnp.zeros((C - 2 * H, C), F32)], axis=0).T.astype(BF)
        w_s[:C] = padded
        w_s[C:] = padded

    u = normalise(z_ref[...].reshape(-1, C))
    both = jnp.concatenate(halves(u), axis=1)
    b = jnp.dot(both, w_s[...], preferred_element_type=F32).T
    return b[:H] + b[H : 2 * H]


def whole_bias_kernel(z_ref, weight_ref, bias_ref, w_s):
    b = bias_rows(z_ref, weight_ref, w_s)
    for at in range(0, b.shape[1], 128):
        bias_ref[at // 128 * H : at // 128 * H + H, :] = b[:, at : at + 128]


def split_bias_kernel(z_ref, weight_ref, keep_ref, send_ref, w_s):
    b = bias_rows(z_ref, weight_ref, w_s)
    first = lax.axis_index("core") == 0
    for row in range(2):
        for block in range(3):
            at = row * N + block * 128
            low = b[:, at : at + 128]
            high = b[:, at + 384 : at + 512]
            to = pl.ds(row * 12 + block * H, H)
            keep_ref[to, :] = jnp.where(first, low, high)
            send_ref[to, :] = jnp.where(first, high, low)


def bias_call(z, bias_weight, split):
    rows = z.shape[0]
    height = 12 if split else 24
    out = jax.ShapeDtypeStruct((rows * height, 128), F32)
    out_spec = pl.BlockSpec((2 * height, 128), lambda r: (r, 0))
    return pl.pallas_call(
        split_bias_kernel if split else whole_bias_kernel,
        grid=(rows // 2,),
        in_specs=[
            pl.BlockSpec((2, N, C), lambda r: (r, 0, 0)),
            pl.BlockSpec((H, C), lambda r: (0, 0)),
        ],
        out_specs=[out_spec, out_spec] if split else out_spec,
        out_shape=[out, out] if split else out,
        scratch_shapes=[pltpu.VMEM((2 * C, C), BF)],
        compiler_params=pltpu.CompilerParams(vmem_limit_bytes=56 * 2**20),
        cost_estimate=pl.CostEstimate(flops=rows * N * C * 20, bytes_accessed=rows * N * C * 4, transcendentals=0),
        name="bias",
    )(z, bias_weight.T)


OFFSETS = (0, 3, 1, 2)


def device_index(y, z, x, core):
    return ((y % 4) * 4 + z % 4) * 8 + (x % 4) * 2 + core


def moves(first, second, step):
    pairs = []
    for y in range(4):
        for z in range(4):
            for x in range(4):
                for core in range(2):
                    axis = (first, second)[core]
                    to = (y + step * (axis == "y"), z + step * (axis == "z"), x + step * (axis == "x"))
                    pairs.append((device_index(y, z, x, core), device_index(*to, core)))
    return pairs


SWAP = [(d, d ^ 1) for d in range(128)]


def ring_gather(keep, send, x, core):
    def move(value, pairs):
        return lax.ppermute(value, AXES, pairs)

    other = move(send, SWAP)
    chip = jnp.where(core == 0, jnp.concatenate([keep, other]), jnp.concatenate([other, keep]))
    before = move(chip, moves("x", "x", 1))
    after = move(chip, moves("x", "x", -1))
    across = move(chip, moves("x", "x", 2))
    size = chip.shape[0]
    line = jnp.concatenate([chip, after, across, before] * 2)
    block = lax.dynamic_slice_in_dim(line, ((4 - x) % 4) * size, 4 * size)

    def along(block, first, second):
        half = block.shape[0] // 2
        up, down = moves(first, second, 1), moves(first, second, -1)
        before, after = move(block, up), move(block, down)
        return [block, before, after, move(before[:half], up), move(after[half:], down)]

    plane = jnp.concatenate([block] + [move(block, moves("z", "y", step)) for step in (1, -1, 2)])
    own = along(plane, "y", "z")
    return own + [move(piece, SWAP) for piece in own]


def project_kernel(carried, valid_ref, z_ref, p_ref, *refs):
    q_ref, k_ref, v_ref, g_ref, w_ref, wg_ref = refs[carried:]
    lane = lax.broadcasted_iota(jnp.int32, (1, C), 1)
    group = lane // D

    @pl.when(pl.program_id(0) == 0)
    def _():
        group_c = lax.broadcasted_iota(jnp.int32, (C, C), 1) // D
        for part in range(3):
            base = p_ref[part]
            if part == 0:
                base = base * (LOG2E * D**-0.5)
            turned = [base] + [pltpu.roll(base, D * m, 1) for m in range(1, 4)]
            for head in range(H):
                block = turned[(0 - head) % H]
                for g in range(1, H):
                    block = jnp.where(group_c == g, turned[(g - head) % H], block)
                high, low = halves(block)
                at = pl.ds((part * H + head) * C, C)
                w_ref[0, :C, at] = high
                w_ref[0, C:, at] = high
                w_ref[1, :C, at] = low
                w_ref[1, C:, at] = low
        high, low = halves(p_ref[3])
        wg_ref[0, :C] = high
        wg_ref[0, C:] = high
        wg_ref[1, :C] = low
        wg_ref[1, C:] = low

    u = normalise(z_ref[0])
    u_high, u_low = halves(u)
    u2 = jnp.concatenate([u_high, u_low], axis=1)

    def project(w):
        return jnp.dot(u2, w[0], preferred_element_type=F32) + jnp.dot(
            u2, w[1], preferred_element_type=F32
        )

    dead = lax.broadcasted_iota(jnp.int32, (N, 1), 0) >= valid_ref[0]
    dead_value = jnp.where(dead, -1e9, 0.0)
    for part in range(3):
        for head in range(H):
            at = pl.ds((part * H + head) * C, C)
            x = project((w_ref[0, :, at], w_ref[1, :, at]))
            high = x.astype(BF).astype(F32)
            low = x - high
            if part == 0:
                out = jnp.where(group == 1, low, high)
                out = jnp.where(group == 3, jnp.where(lane == 3 * D, 1.0, 0.0), out)
                q_ref[0, head] = out.astype(BF)
            elif part == 1:
                out = jnp.where(group == 2, low, high)
                out = jnp.where(group == 3, jnp.where(lane == 3 * D, dead_value, 0.0), out)
                k_ref[0, head] = out.astype(BF)
            else:
                out = jnp.where(group == (head + 1) % H, low, high)
                out = jnp.where(group == (head + 2) % H, 1.0, out)
                out = jnp.where(group == (head + 3) % H, 0.0, out)
                v_ref[0, head] = out.astype(BF)
    g_ref[0] = jax.nn.sigmoid(project((wg_ref[0], wg_ref[1])))


def project_call(z, projection, valid_count, first, count, carry):
    rows = z.shape[0]
    heads = jax.ShapeDtypeStruct((rows, H, N, C), BF)
    head_spec = pl.BlockSpec((1, H, N, C), lambda r, s: (r + first, 0, 0, 0))
    row_spec = pl.BlockSpec((1, N, C), lambda r, s: (r + first, 0, 0))
    carry = carry or []
    return pl.pallas_call(
        functools.partial(project_kernel, len(carry)),
        grid_spec=pltpu.PrefetchScalarGridSpec(
            num_scalar_prefetch=1,
            grid=(count,),
            in_specs=[row_spec, pl.BlockSpec((4, C, C), lambda r, s: (0, 0, 0))]
            + [pl.BlockSpec(memory_space=pl.ANY)] * len(carry),
            out_specs=[head_spec, head_spec, head_spec, row_spec],
            scratch_shapes=[
                pltpu.VMEM((2, 2 * C, 3 * H * C), BF),
                pltpu.VMEM((2, 2 * C, C), BF),
            ],
        ),
        out_shape=[heads, heads, heads, jax.ShapeDtypeStruct((rows, N, C), F32)],
        input_output_aliases={3 + n: n for n in range(len(carry))},
        compiler_params=pltpu.CompilerParams(vmem_limit_bytes=56 * 2**20),
        cost_estimate=pl.CostEstimate(
            flops=count * N * 2 * C * 2 * 13 * C * 8, bytes_accessed=count * N * C * 4 * 8, transcendentals=0
        ),
        name="project",
    )(valid_count, z, projection, *carry)


def project_all(z, projection, valid_count, parts):
    carry = None
    size = z.shape[0] // parts
    for part in range(parts):
        carry = project_call(z, projection, valid_count, part * size, size, carry)
    return carry


def attend_kernel(rows, QC, KT, transposed, valid_ref, q_ref, k_ref, v_ref, g_ref, z_ref, o_ref, *refs):
    *bias_refs, out_ref, bias_s, acc_s, o_s = refs
    group = lax.broadcasted_iota(jnp.int32, (1, C), 1) // D
    chunk, row = pl.program_id(0), pl.program_id(1)
    per = N // 128 * H

    @pl.when((chunk == 0) & (row == 0))
    def _():
        high, low = halves(o_ref[...])
        o_s[0, :C] = high
        o_s[0, C:] = high
        o_s[1, :C] = low
        o_s[1, C:] = low

    @pl.when(row == 0)
    def _():
        if transposed:
            bias_ref = bias_refs[0]
            for head in range(H):
                for block in range(N // 128):
                    for part in range(QC // 128):
                        first = block * 128 * per + (chunk * (QC // 128) + part) * H + head
                        tile = bias_ref[pl.ds(first, 128, stride=per), :]
                        bias_s[head, block, pl.ds(part * 128, 128), :] = tile.T
        else:
            my_y, my_z, core = lax.axis_index("y"), lax.axis_index(("z_hi", "z_lo")), lax.axis_index("core")
            per_half = per // 2
            size = 48 * per_half
            for side in range(2):
                half = core if side == 0 else 1 - core
                pieces = bias_refs[side * 5 : side * 5 + 5]
                for last, last_step in enumerate(OFFSETS):
                    for mid, mid_step in enumerate(OFFSETS):
                        y_step = jnp.where(half == 0, last_step, mid_step)
                        z_step = jnp.where(half == 0, mid_step, last_step)
                        to = ((my_y + y_step) % 4) * 192 + ((my_z + z_step) % 4) * 48
                        to = pl.ds(pl.multiple_of(to, 48), 48)
                        piece, place = (pieces[last], mid) if last < 3 else (pieces[3 + mid // 2], mid % 2)
                        for head in range(H):
                            for block in range(3):
                                bias_s[head, half * 3 + block, to, :] = piece[
                                    pl.ds(place * size + block * H + head, 48, stride=per_half), :
                                ]

    def bias_of(head, at, size):
        blocks = [bias_s[head, (at + b) // 128] for b in range(0, size, 128)]
        return blocks[0] if len(blocks) == 1 else jnp.concatenate(blocks, axis=1)

    def finish():
        slot = (row + 1) % 2
        value = low_value = total = None
        for head in range(H):
            acc = acc_s[slot, head]
            if head == 0:
                value = low_value = total = acc
            else:
                value = jnp.where(group == head, acc, value)
                low_value = jnp.where(group == (head + 1) % H, acc, low_value)
                total = jnp.where(group == (head + 2) % H, acc, total)
        value = value + pltpu.roll(low_value, 3 * D, 1)
        mixed = value / pltpu.roll(total, 2 * D, 1) * g_ref[0]
        high, low = halves(mixed)
        both = jnp.concatenate([high, low], axis=1)
        out_ref[0] = (
            z_ref[0]
            + jnp.dot(both, o_s[0], preferred_element_type=F32)
            + jnp.dot(both, o_s[1], preferred_element_type=F32)
        )

    def run(keys):
        for head in range(H):
            q = q_ref[0, head]
            acc = None
            for at in range(0, keys, KT):
                size = min(KT, keys - at)
                s = lax.dot_general(
                    q, k_ref[0, head, at : at + size, :], (((1,), (1,)), ((), ())),
                    preferred_element_type=F32,
                )
                w = jnp.exp2(s + bias_of(head, at, size))
                high, low = halves(w)
                v = v_ref[0, head, at : at + size, :]
                term = jnp.dot(high, v, preferred_element_type=F32) + jnp.dot(
                    low, v, preferred_element_type=F32
                )
                acc = term if acc is None else acc + term
            acc_s[row % 2, head] = acc

    count = (valid_ref[0] + 127) // 128
    for blocks in range(3, N // 128 + 1):

        @pl.when((count == blocks) & (row < rows))
        def _():
            run(blocks * 128)
            finish()

    @pl.when(row == rows)
    def _():
        finish()


def attend_call(q, k, v, g, z, bias, out_weight, valid_count, QC=N, KT=256, transposed=False):
    rows = z.shape[0]
    queries = z.shape[1]
    now = lambda r: jnp.minimum(r, rows - 1)
    last = lambda r: jnp.maximum(r - 1, 0)
    key_spec = pl.BlockSpec((1, H, N, C), lambda c, r, s: (now(r), 0, 0, 0))
    row_spec = pl.BlockSpec((1, QC, C), lambda c, r, s: (last(r), c, 0))
    bias_specs = [
        pl.BlockSpec(piece.shape, lambda c, r, s: (0, 0), pipeline_mode=pl.Buffered(1)) for piece in bias
    ]
    return pl.pallas_call(
        functools.partial(attend_kernel, rows, QC, KT, transposed),
        grid_spec=pltpu.PrefetchScalarGridSpec(
            num_scalar_prefetch=1,
            grid=(queries // QC, rows + 1),
            in_specs=[
                pl.BlockSpec((1, H, QC, C), lambda c, r, s: (now(r), 0, c, 0)),
                key_spec,
                key_spec,
                row_spec,
                row_spec,
                pl.BlockSpec((C, C), lambda c, r, s: (0, 0)),
                *bias_specs,
            ],
            out_specs=row_spec,
            scratch_shapes=[
                pltpu.VMEM((H, N // 128, QC, 128), F32),
                pltpu.VMEM((2, H, QC, C), F32),
                pltpu.VMEM((2, 2 * C, C), BF),
            ],
        ),
        out_shape=jax.ShapeDtypeStruct(z.shape, F32),
        compiler_params=pltpu.CompilerParams(vmem_limit_bytes=56 * 2**20),
        cost_estimate=pl.CostEstimate(
            flops=rows * queries * N * H * 64 * 4, bytes_accessed=rows * N * C * 4 * 8, transcendentals=0
        ),
        name="attend",
    )(valid_count, q, k, v, g, z, out_weight, *bias)


def per_device(
    pair_rows, valid_count, start_proj, start_out, start_bias, end_proj, end_out, end_bias
):
    keep, send = bias_call(pair_rows, start_bias, True)
    pieces = ring_gather(keep, send, lax.axis_index("x"), lax.axis_index("core"))
    q, k, v, g = project_all(pair_rows, start_proj, valid_count, 3)
    updated = attend_call(q, k, v, g, pair_rows, pieces, start_out, valid_count)
    end_gathered = lax.all_gather(bias_call(updated, end_bias, False), AXES, axis=0, tiled=True)
    columns = lax.all_to_all(updated, AXES, split_axis=1, concat_axis=0, tiled=True)
    turned = jnp.swapaxes(columns, 0, 1)
    q, k, v, g = project_all(turned, end_proj, valid_count, 1)
    return attend_call(q, k, v, g, turned, [end_gathered], end_out, valid_count, transposed=True)


def solution(mesh):
    fine = Mesh(mesh.devices.reshape(4, 2, 2, 4, 2), AXES)
    return jax.shard_map(
        per_device,
        mesh=fine,
        in_specs=(P(AXES, None, None), P(), P(), P(), P(), P(), P(), P()),
        out_specs=P(AXES, None, None),
        check_vma=False,
    )
```

```python
import functools
import jax
import jax.numpy as jnp
from jax import lax
from jax.sharding import PartitionSpec as P
from jax.experimental import pallas as pl
from jax.experimental.pallas import tpu as pltpu

LOG2E = 1.4426950408889634
BF = jnp.bfloat16
F32 = jnp.float32
HIGHEST = lax.Precision.HIGHEST
AXES = ("row", "col")
ROWS, N, C, H, D = 6, 768, 128, 4, 32


def normalise(values):
    average = jnp.mean(values, axis=-1, keepdims=True)
    centred = values - average
    variance = jnp.mean(centred * centred, axis=-1, keepdims=True)
    return centred * lax.rsqrt(variance + 1e-05)


def halves(values):
    high = values.astype(BF)
    return high, (values - high.astype(F32)).astype(BF)


def prepare_bias(weight_ref, w_s):
    weight = weight_ref[...] * LOG2E
    high = weight.astype(BF).astype(F32)
    padded = jnp.concatenate([high, weight - high, jnp.zeros((C - 2 * H, C), F32)], axis=0).T.astype(BF)
    w_s[:C] = padded
    w_s[C:] = padded


def project_bias(values, w_s):
    both = jnp.concatenate(halves(normalise(values)), axis=1)
    b = jnp.dot(both, w_s[...], preferred_element_type=F32).T
    return b[:H] + b[H : 2 * H]


def bias_kernel(z_ref, weight_ref, bias_ref, w_s):
    @pl.when(pl.program_id(0) == 0)
    def _():
        prepare_bias(weight_ref, w_s)

    b = project_bias(z_ref[...].reshape(2 * N, C), w_s)
    for row in range(2):
        store_bias(bias_ref, row, b[:, row * N : (row + 1) * N])


def store_bias(bias_ref, row, b):
    for block in range(N // 128):
        at = (row * (N // 128) + block) * H
        bias_ref[at : at + H, :] = b[:, block * 128 : (block + 1) * 128]


def bias_call(z, bias_weight):
    rows = z.shape[0]
    return pl.pallas_call(
        bias_kernel,
        grid=(rows // 2,),
        in_specs=[
            pl.BlockSpec((2, N, C), lambda r: (r, 0, 0)),
            pl.BlockSpec((H, C), lambda r: (0, 0)),
        ],
        out_specs=pl.BlockSpec((48, 128), lambda r: (r, 0)),
        out_shape=jax.ShapeDtypeStruct((rows * 24, 128), F32),
        scratch_shapes=[pltpu.VMEM((2 * C, C), BF)],
        compiler_params=pltpu.CompilerParams(vmem_limit_bytes=56 * 2**20),
        cost_estimate=pl.CostEstimate(flops=rows * N * C * 20, bytes_accessed=rows * N * C * 4, transcendentals=0),
        name="bias",
    )(z, bias_weight.T)


def project_kernel(carried, valid_ref, z_ref, p_ref, *refs):
    q_ref, k_ref, v_ref, g_ref, w_ref, wg_ref = refs[carried:]
    lane = lax.broadcasted_iota(jnp.int32, (1, C), 1)
    group = lane // D

    @pl.when(pl.program_id(0) == 0)
    def _():
        group_c = lax.broadcasted_iota(jnp.int32, (C, C), 1) // D
        for part in range(3):
            base = p_ref[part]
            if part == 0:
                base = base * (LOG2E * D**-0.5)
            turned = [base] + [pltpu.roll(base, D * m, 1) for m in range(1, 4)]
            for head in range(H):
                block = turned[(0 - head) % H]
                for g in range(1, H):
                    block = jnp.where(group_c == g, turned[(g - head) % H], block)
                high, low = halves(block)
                at = pl.ds((part * H + head) * C, C)
                w_ref[0, :C, at] = high
                w_ref[0, C:, at] = high
                w_ref[1, :C, at] = low
                w_ref[1, C:, at] = low
        high, low = halves(p_ref[3])
        wg_ref[0, :C] = high
        wg_ref[0, C:] = high
        wg_ref[1, :C] = low
        wg_ref[1, C:] = low

    u = normalise(z_ref[0])
    u_high, u_low = halves(u)
    u2 = jnp.concatenate([u_high, u_low], axis=1)

    def project(w):
        return jnp.dot(u2, w[0], preferred_element_type=F32) + jnp.dot(
            u2, w[1], preferred_element_type=F32
        )

    dead = lax.broadcasted_iota(jnp.int32, (N, 1), 0) >= valid_ref[0]
    dead_value = jnp.where(dead, -1e9, 0.0)
    for part in range(3):
        for head in range(H):
            at = pl.ds((part * H + head) * C, C)
            x = project((w_ref[0, :, at], w_ref[1, :, at]))
            high = x.astype(BF).astype(F32)
            low = x - high
            if part == 0:
                out = jnp.where(group == 1, low, high)
                out = jnp.where(group == 3, jnp.where(lane == 3 * D, 1.0, 0.0), out)
                q_ref[0, head] = out.astype(BF)
            elif part == 1:
                out = jnp.where(group == 2, low, high)
                out = jnp.where(group == 3, jnp.where(lane == 3 * D, dead_value, 0.0), out)
                k_ref[0, head] = out.astype(BF)
            else:
                out = jnp.where(group == (head + 1) % H, low, high)
                out = jnp.where(group == (head + 2) % H, 1.0, out)
                out = jnp.where(group == (head + 3) % H, 0.0, out)
                v_ref[0, head] = out.astype(BF)
    g_ref[0] = jax.nn.sigmoid(project((wg_ref[0], wg_ref[1])))


def project_call(z, projection, valid_count, first, count, carry):
    rows = z.shape[0]
    heads = jax.ShapeDtypeStruct((rows, H, N, C), BF)
    head_spec = pl.BlockSpec((1, H, N, C), lambda r, s: (r + first, 0, 0, 0))
    row_spec = pl.BlockSpec((1, N, C), lambda r, s: (r + first, 0, 0))
    carry = carry or []
    return pl.pallas_call(
        functools.partial(project_kernel, len(carry)),
        grid_spec=pltpu.PrefetchScalarGridSpec(
            num_scalar_prefetch=1,
            grid=(count,),
            in_specs=[row_spec, pl.BlockSpec((4, C, C), lambda r, s: (0, 0, 0))]
            + [pl.BlockSpec(memory_space=pl.ANY)] * len(carry),
            out_specs=[head_spec, head_spec, head_spec, row_spec],
            scratch_shapes=[
                pltpu.VMEM((2, 2 * C, 3 * H * C), BF),
                pltpu.VMEM((2, 2 * C, C), BF),
            ],
        ),
        out_shape=[heads, heads, heads, jax.ShapeDtypeStruct((rows, N, C), F32)],
        input_output_aliases={3 + n: n for n in range(len(carry))},
        compiler_params=pltpu.CompilerParams(vmem_limit_bytes=56 * 2**20),
        cost_estimate=pl.CostEstimate(
            flops=count * N * 2 * C * 2 * 13 * C * 8, bytes_accessed=count * N * C * 4 * 8, transcendentals=0
        ),
        name="project",
    )(valid_count, z, projection, *carry)


def project_all(z, projection, valid_count, parts):
    carry = None
    size = z.shape[0] // parts
    for part in range(parts):
        carry = project_call(z, projection, valid_count, part * size, size, carry)
    return carry


def attend_kernel(rows, KT, transposed, with_bias, valid_ref, q_ref, k_ref, v_ref, g_ref, z_ref, o_ref, bias_ref,
                  *refs):
    if with_bias:
        weight_ref, out_ref, local_ref, bias_s, acc_s, o_s, w_s, b_s = refs
    else:
        out_ref, bias_s, acc_s, o_s = refs
    group = lax.broadcasted_iota(jnp.int32, (1, C), 1) // D
    step = pl.program_id(0)
    per = N // 128 * H

    @pl.when(step == 0)
    def _():
        high, low = halves(o_ref[...])
        o_s[0, :C] = high
        o_s[0, C:] = high
        o_s[1, :C] = low
        o_s[1, C:] = low
        if with_bias:
            prepare_bias(weight_ref, w_s)

    @pl.when(step == 0)
    def _():
        for head in range(H):
            for block in range(N // 128):
                at = pl.ds(block * 128, 128)
                if transposed:
                    for part in range(N // 128):
                        tile = bias_ref[pl.ds(block * 128 * per + part * H + head, 128, stride=per), :]
                        bias_s[head, pl.ds(part * 128, 128), at] = tile.T
                else:
                    bias_s[head, :, at] = bias_ref[pl.ds(block * H + head, N, stride=per), :]

    def attend(head, keys):
        q = q_ref[0, head]
        acc = None
        for at in range(0, keys, KT):
            size = min(KT, keys - at)
            s = lax.dot_general(
                q, k_ref[0, head, at : at + size, :], (((1,), (1,)), ((), ())),
                preferred_element_type=F32,
            )
            w = jnp.exp2(s + bias_s[head, :, at : at + size])
            high, low = halves(w)
            v = v_ref[0, head, at : at + size, :]
            term = jnp.dot(high, v, preferred_element_type=F32) + jnp.dot(
                low, v, preferred_element_type=F32
            )
            acc = term if acc is None else acc + term
        acc_s[step % 2, head] = acc

    def finish():
        row = jnp.maximum(step - 1, 0)
        value = low_value = total = None
        for head in range(H):
            acc = acc_s[(step + 1) % 2, head]
            if head == 0:
                value = low_value = total = acc
            else:
                value = jnp.where(group == head, acc, value)
                low_value = jnp.where(group == (head + 1) % H, acc, low_value)
                total = jnp.where(group == (head + 2) % H, acc, total)
        value = value + pltpu.roll(low_value, 3 * D, 1)
        mixed = value / pltpu.roll(total, 2 * D, 1) * g_ref[0]
        high, low = halves(mixed)
        both = jnp.concatenate([high, low], axis=1)
        updated = (
            z_ref[0]
            + jnp.dot(both, o_s[0], preferred_element_type=F32)
            + jnp.dot(both, o_s[1], preferred_element_type=F32)
        )
        out_ref[0] = updated
        if with_bias:
            b_s[row, :H] = project_bias(updated, w_s)

    count = (valid_ref[0] + 127) // 128
    for blocks in range(3, N // 128 + 1):

        @pl.when((count == blocks) & (step < rows))
        def _():
            finish()
            for head in range(H):
                attend(head, blocks * 128)

    @pl.when(step == rows)
    def _():
        finish()
        if with_bias:
            for row in range(rows):
                store_bias(local_ref, row, b_s[row, :H])


def attend_call(q, k, v, g, z, bias, out_weight, valid_count, next_bias=None, KT=256, transposed=False):
    rows = z.shape[0]

    def now(t):
        return jnp.minimum(t, rows - 1)

    def last(t):
        return jnp.maximum(t - 1, 0)

    key_spec = pl.BlockSpec((1, H, N, C), lambda t, s: (now(t), 0, 0, 0))
    row_spec = pl.BlockSpec((1, N, C), lambda t, s: (last(t), 0, 0))
    in_specs = [
        key_spec,
        key_spec,
        key_spec,
        row_spec,
        row_spec,
        pl.BlockSpec((C, C), lambda t, s: (0, 0)),
        pl.BlockSpec((N * N // 128 * H, 128), lambda t, s: (0, 0), pipeline_mode=pl.Buffered(1)),
    ]
    out_specs = [row_spec]
    out_shape = [jax.ShapeDtypeStruct(z.shape, F32)]
    scratch = [
        pltpu.VMEM((H, N, N), F32),
        pltpu.VMEM((2, H, N, C), F32),
        pltpu.VMEM((2, 2 * C, C), BF),
    ]
    args = [q, k, v, g, z, out_weight, bias]
    if next_bias is not None:
        in_specs.append(pl.BlockSpec((H, C), lambda t, s: (0, 0)))
        args.append(next_bias.T)
        out_specs.append(pl.BlockSpec((rows * 24, 128), lambda t, s: (0, 0)))
        out_shape.append(jax.ShapeDtypeStruct((rows * 24, 128), F32))
        scratch += [pltpu.VMEM((2 * C, C), BF), pltpu.VMEM((rows, 8, N), F32)]
    return pl.pallas_call(
        functools.partial(attend_kernel, rows, KT, transposed, next_bias is not None),
        grid_spec=pltpu.PrefetchScalarGridSpec(
            num_scalar_prefetch=1,
            grid=(rows + 1,),
            in_specs=in_specs,
            out_specs=out_specs,
            scratch_shapes=scratch,
        ),
        out_shape=out_shape,
        compiler_params=pltpu.CompilerParams(vmem_limit_bytes=56 * 2**20),
        cost_estimate=pl.CostEstimate(
            flops=rows * N * N * H * 64 * 4, bytes_accessed=rows * N * C * 4 * 8, transcendentals=0
        ),
        name="attend",
    )(valid_count, *args)


def per_device(
    pair_rows, valid_count, start_proj, start_out, start_bias, end_proj, end_out, end_bias
):
    def gather(local):
        return lax.all_gather(local, AXES, axis=0, tiled=True)

    start_gathered = gather(bias_call(pair_rows, start_bias))
    q, k, v, g = project_all(pair_rows, start_proj, valid_count, 1)
    updated, local = attend_call(q, k, v, g, pair_rows, start_gathered, start_out, valid_count, end_bias)
    end_gathered = gather(local)
    columns = lax.all_to_all(updated, AXES, split_axis=1, concat_axis=0, tiled=True)
    turned = jnp.swapaxes(columns, 0, 1)
    q, k, v, g = project_all(turned, end_proj, valid_count, 1)
    return attend_call(q, k, v, g, turned, end_gathered, end_out, valid_count, transposed=True)[0]


def solution(mesh):
    return jax.shard_map(
        per_device,
        mesh=mesh,
        in_specs=(P(AXES, None, None), P(), P(), P(), P(), P(), P(), P()),
        out_specs=P(AXES, None, None),
        check_vma=False,
    )
```

```python
import functools
import jax
import jax.numpy as jnp
from jax import lax
from jax.sharding import PartitionSpec as P
from jax.experimental import pallas as pl
from jax.experimental.pallas import tpu as pltpu

LOG2E = 1.4426950408889634
BF = jnp.bfloat16
F32 = jnp.float32
HIGHEST = lax.Precision.HIGHEST
AXES = ("row", "col")
ROWS, N, C, H, D = 6, 768, 128, 4, 32


def normalise(values):
    average = jnp.mean(values, axis=-1, keepdims=True)
    centred = values - average
    variance = jnp.mean(centred * centred, axis=-1, keepdims=True)
    return centred * lax.rsqrt(variance + 1e-05)


def halves(values):
    high = values.astype(BF)
    return high, (values - high.astype(F32)).astype(BF)


def prepare_bias(weight_ref, w_s):
    weight = weight_ref[...] * LOG2E
    high = weight.astype(BF).astype(F32)
    padded = jnp.concatenate([high, weight - high, jnp.zeros((C - 2 * H, C), F32)], axis=0).T.astype(BF)
    w_s[:C] = padded
    w_s[C:] = padded


def project_bias(values, w_s):
    both = jnp.concatenate(halves(normalise(values)), axis=1)
    b = jnp.dot(both, w_s[...], preferred_element_type=F32).T
    return b[:H] + b[H : 2 * H]


def bias_kernel(z_ref, weight_ref, bias_ref, w_s):
    @pl.when(pl.program_id(0) == 0)
    def _():
        prepare_bias(weight_ref, w_s)

    b = project_bias(z_ref[...].reshape(2 * N, C), w_s)
    for row in range(2):
        store_bias(bias_ref, row, b[:, row * N : (row + 1) * N])


def store_bias(bias_ref, row, b):
    for block in range(N // 128):
        at = (row * (N // 128) + block) * H
        bias_ref[at : at + H, :] = b[:, block * 128 : (block + 1) * 128]


def bias_call(z, bias_weight):
    rows = z.shape[0]
    return pl.pallas_call(
        bias_kernel,
        grid=(rows // 2,),
        in_specs=[
            pl.BlockSpec((2, N, C), lambda r: (r, 0, 0)),
            pl.BlockSpec((H, C), lambda r: (0, 0)),
        ],
        out_specs=pl.BlockSpec((48, 128), lambda r: (r, 0)),
        out_shape=jax.ShapeDtypeStruct((rows * 24, 128), F32),
        scratch_shapes=[pltpu.VMEM((2 * C, C), BF)],
        compiler_params=pltpu.CompilerParams(vmem_limit_bytes=56 * 2**20),
        cost_estimate=pl.CostEstimate(flops=rows * N * C * 20, bytes_accessed=rows * N * C * 4, transcendentals=0),
        name="bias",
    )(z, bias_weight.T)


def project_kernel(carried, valid_ref, z_ref, p_ref, *refs):
    q_ref, k_ref, v_ref, g_ref, w_ref, wg_ref = refs[carried:]
    lane = lax.broadcasted_iota(jnp.int32, (1, C), 1)
    group = lane // D

    @pl.when(pl.program_id(0) == 0)
    def _():
        group_c = lax.broadcasted_iota(jnp.int32, (C, C), 1) // D
        for part in range(3):
            base = p_ref[part]
            if part == 0:
                base = base * (LOG2E * D**-0.5)
            turned = [base] + [pltpu.roll(base, D * m, 1) for m in range(1, 4)]
            for head in range(H):
                block = turned[(0 - head) % H]
                for g in range(1, H):
                    block = jnp.where(group_c == g, turned[(g - head) % H], block)
                high, low = halves(block)
                at = pl.ds((part * H + head) * C, C)
                w_ref[0, :C, at] = high
                w_ref[0, C:, at] = high
                w_ref[1, :C, at] = low
                w_ref[1, C:, at] = low
        high, low = halves(p_ref[3])
        wg_ref[0, :C] = high
        wg_ref[0, C:] = high
        wg_ref[1, :C] = low
        wg_ref[1, C:] = low

    u = normalise(z_ref[0])
    u_high, u_low = halves(u)
    u2 = jnp.concatenate([u_high, u_low], axis=1)

    def project(w):
        return jnp.dot(u2, w[0], preferred_element_type=F32) + jnp.dot(
            u2, w[1], preferred_element_type=F32
        )

    dead = lax.broadcasted_iota(jnp.int32, (N, 1), 0) >= valid_ref[0]
    dead_value = jnp.where(dead, -1e9, 0.0)
    for part in range(3):
        for head in range(H):
            at = pl.ds((part * H + head) * C, C)
            x = project((w_ref[0, :, at], w_ref[1, :, at]))
            high = x.astype(BF).astype(F32)
            low = x - high
            if part == 0:
                out = jnp.where(group == 1, low, high)
                out = jnp.where(group == 3, jnp.where(lane == 3 * D, 1.0, 0.0), out)
                q_ref[0, head] = out.astype(BF)
            elif part == 1:
                out = jnp.where(group == 2, low, high)
                out = jnp.where(group == 3, jnp.where(lane == 3 * D, dead_value, 0.0), out)
                k_ref[0, head] = out.astype(BF)
            else:
                out = jnp.where(group == (head + 1) % H, low, high)
                out = jnp.where(group == (head + 2) % H, 1.0, out)
                out = jnp.where(group == (head + 3) % H, 0.0, out)
                v_ref[0, head] = out.astype(BF)
    g_ref[0] = jax.nn.sigmoid(project((wg_ref[0], wg_ref[1])))


def project_call(z, projection, valid_count, first, count, carry):
    rows = z.shape[0]
    heads = jax.ShapeDtypeStruct((rows, H, N, C), BF)
    head_spec = pl.BlockSpec((1, H, N, C), lambda r, s: (r + first, 0, 0, 0))
    row_spec = pl.BlockSpec((1, N, C), lambda r, s: (r + first, 0, 0))
    carry = carry or []
    return pl.pallas_call(
        functools.partial(project_kernel, len(carry)),
        grid_spec=pltpu.PrefetchScalarGridSpec(
            num_scalar_prefetch=1,
            grid=(count,),
            in_specs=[row_spec, pl.BlockSpec((4, C, C), lambda r, s: (0, 0, 0))]
            + [pl.BlockSpec(memory_space=pl.ANY)] * len(carry),
            out_specs=[head_spec, head_spec, head_spec, row_spec],
            scratch_shapes=[
                pltpu.VMEM((2, 2 * C, 3 * H * C), BF),
                pltpu.VMEM((2, 2 * C, C), BF),
            ],
        ),
        out_shape=[heads, heads, heads, jax.ShapeDtypeStruct((rows, N, C), F32)],
        input_output_aliases={3 + n: n for n in range(len(carry))},
        compiler_params=pltpu.CompilerParams(vmem_limit_bytes=56 * 2**20),
        cost_estimate=pl.CostEstimate(
            flops=count * N * 2 * C * 2 * 13 * C * 8, bytes_accessed=count * N * C * 4 * 8, transcendentals=0
        ),
        name="project",
    )(valid_count, z, projection, *carry)


def project_all(z, projection, valid_count, parts):
    carry = None
    size = z.shape[0] // parts
    for part in range(parts):
        carry = project_call(z, projection, valid_count, part * size, size, carry)
    return carry


def attend_kernel(rows, KT, transposed, with_bias, valid_ref, q_ref, k_ref, v_ref, g_ref, z_ref, o_ref, bias_ref,
                  *refs):
    if with_bias:
        weight_ref, out_ref, local_ref, bias_s, acc_s, o_s, w_s, b_s = refs
    else:
        out_ref, bias_s, acc_s, o_s = refs
    group = lax.broadcasted_iota(jnp.int32, (1, C), 1) // D
    step = pl.program_id(0)
    per = N // 128 * H

    @pl.when(step == 0)
    def _():
        high, low = halves(o_ref[...])
        o_s[0, :C] = high
        o_s[0, C:] = high
        o_s[1, :C] = low
        o_s[1, C:] = low
        if with_bias:
            prepare_bias(weight_ref, w_s)

    @pl.when(step == 0)
    def _():
        for head in range(H):
            for block in range(N // 128):
                at = pl.ds(block * 128, 128)
                if transposed:
                    for part in range(N // 128):
                        tile = bias_ref[pl.ds(block * 128 * per + part * H + head, 128, stride=per), :]
                        bias_s[head, pl.ds(part * 128, 128), at] = tile.T
                else:
                    bias_s[head, :, at] = bias_ref[pl.ds(block * H + head, N, stride=per), :]

    def attend(head, keys):
        q = q_ref[0, head]
        acc = None
        for at in range(0, keys, KT):
            size = min(KT, keys - at)
            s = lax.dot_general(
                q, k_ref[0, head, at : at + size, :], (((1,), (1,)), ((), ())),
                preferred_element_type=F32,
            )
            w = jnp.exp2(s + bias_s[head, :, at : at + size])
            high, low = halves(w)
            v = v_ref[0, head, at : at + size, :]
            term = jnp.dot(high, v, preferred_element_type=F32) + jnp.dot(
                low, v, preferred_element_type=F32
            )
            acc = term if acc is None else acc + term
        acc_s[step % 2, head] = acc

    def finish():
        row = jnp.maximum(step - 1, 0)
        value = low_value = total = None
        for head in range(H):
            acc = acc_s[(step + 1) % 2, head]
            if head == 0:
                value = low_value = total = acc
            else:
                value = jnp.where(group == head, acc, value)
                low_value = jnp.where(group == (head + 1) % H, acc, low_value)
                total = jnp.where(group == (head + 2) % H, acc, total)
        value = value + pltpu.roll(low_value, 3 * D, 1)
        mixed = value / pltpu.roll(total, 2 * D, 1) * g_ref[0]
        high, low = halves(mixed)
        both = jnp.concatenate([high, low], axis=1)
        updated = (
            z_ref[0]
            + jnp.dot(both, o_s[0], preferred_element_type=F32)
            + jnp.dot(both, o_s[1], preferred_element_type=F32)
        )
        out_ref[0] = updated
        if with_bias:
            b_s[row, :H] = project_bias(updated, w_s)

    count = (valid_ref[0] + 127) // 128
    for blocks in range(3, N // 128 + 1):

        @pl.when((count == blocks) & (step < rows))
        def _():
            finish()
            for head in range(H):
                attend(head, blocks * 128)

    @pl.when(step == rows)
    def _():
        finish()
        if with_bias:
            for row in range(rows):
                store_bias(local_ref, row, b_s[row, :H])


def attend_call(q, k, v, g, z, bias, out_weight, valid_count, next_bias=None, KT=256, transposed=False):
    rows = z.shape[0]

    def now(t):
        return jnp.minimum(t, rows - 1)

    def last(t):
        return jnp.maximum(t - 1, 0)

    key_spec = pl.BlockSpec((1, H, N, C), lambda t, s: (now(t), 0, 0, 0))
    row_spec = pl.BlockSpec((1, N, C), lambda t, s: (last(t), 0, 0))
    in_specs = [
        key_spec,
        key_spec,
        key_spec,
        row_spec,
        row_spec,
        pl.BlockSpec((C, C), lambda t, s: (0, 0)),
        pl.BlockSpec((N * N // 128 * H, 128), lambda t, s: (0, 0), pipeline_mode=pl.Buffered(1)),
    ]
    out_specs = [row_spec]
    out_shape = [jax.ShapeDtypeStruct(z.shape, F32)]
    scratch = [
        pltpu.VMEM((H, N, N), F32),
        pltpu.VMEM((2, H, N, C), F32),
        pltpu.VMEM((2, 2 * C, C), BF),
    ]
    args = [q, k, v, g, z, out_weight, bias]
    if next_bias is not None:
        in_specs.append(pl.BlockSpec((H, C), lambda t, s: (0, 0)))
        args.append(next_bias.T)
        out_specs.append(pl.BlockSpec((rows * 24, 128), lambda t, s: (0, 0)))
        out_shape.append(jax.ShapeDtypeStruct((rows * 24, 128), F32))
        scratch += [pltpu.VMEM((2 * C, C), BF), pltpu.VMEM((rows, 8, N), F32)]
    return pl.pallas_call(
        functools.partial(attend_kernel, rows, KT, transposed, next_bias is not None),
        grid_spec=pltpu.PrefetchScalarGridSpec(
            num_scalar_prefetch=1,
            grid=(rows + 1,),
            in_specs=in_specs,
            out_specs=out_specs,
            scratch_shapes=scratch,
        ),
        out_shape=out_shape,
        compiler_params=pltpu.CompilerParams(vmem_limit_bytes=56 * 2**20),
        cost_estimate=pl.CostEstimate(
            flops=rows * N * N * H * 64 * 4, bytes_accessed=rows * N * C * 4 * 8, transcendentals=0
        ),
        name="attend",
    )(valid_count, *args)


def exchange(rows):
    mine, length, width = rows.shape
    parts = length // mine
    sent = rows.reshape(mine, parts, mine, width).transpose(1, 2, 0, 3).reshape(parts, -1, 4, width)
    got = lax.all_to_all(sent, AXES, split_axis=0, concat_axis=0, tiled=True)
    return got.reshape(parts, mine, mine, width).transpose(1, 0, 2, 3).reshape(mine, length, width)


def per_device(
    pair_rows, valid_count, start_proj, start_out, start_bias, end_proj, end_out, end_bias
):
    def gather(local):
        return lax.all_gather(local, AXES, axis=0, tiled=True)

    start_gathered = gather(bias_call(pair_rows, start_bias))
    q, k, v, g = project_all(pair_rows, start_proj, valid_count, 1)
    updated, local = attend_call(q, k, v, g, pair_rows, start_gathered, start_out, valid_count, end_bias)
    end_gathered = gather(local)
    turned = exchange(updated)
    q, k, v, g = project_all(turned, end_proj, valid_count, 1)
    return attend_call(q, k, v, g, turned, end_gathered, end_out, valid_count, transposed=True)[0]


def solution(mesh):
    return jax.shard_map(
        per_device,
        mesh=mesh,
        in_specs=(P(AXES, None, None), P(), P(), P(), P(), P(), P(), P()),
        out_specs=P(AXES, None, None),
        check_vma=False,
    )
```

```python
import functools
import jax
import jax.numpy as jnp
from jax import lax
from jax.sharding import PartitionSpec as P
from jax.experimental import pallas as pl
from jax.experimental.pallas import tpu as pltpu

LOG2E = 1.4426950408889634
BF = jnp.bfloat16
F32 = jnp.float32
HIGHEST = lax.Precision.HIGHEST
AXES = ("row", "col")
ROWS, N, C, H, D = 6, 768, 128, 4, 32


def normalise(values):
    average = jnp.mean(values, axis=-1, keepdims=True)
    centred = values - average
    variance = jnp.mean(centred * centred, axis=-1, keepdims=True)
    return centred * lax.rsqrt(variance + 1e-05)


def halves(values):
    high = values.astype(BF)
    return high, (values - high.astype(F32)).astype(BF)


def prepare_bias(weight_ref, w_s):
    weight = weight_ref[...] * LOG2E
    high = weight.astype(BF).astype(F32)
    padded = jnp.concatenate([high, weight - high, jnp.zeros((C - 2 * H, C), F32)], axis=0).T.astype(BF)
    w_s[:C] = padded
    w_s[C:] = padded


def project_bias(values, w_s):
    both = jnp.concatenate(halves(normalise(values)), axis=1)
    b = jnp.dot(both, w_s[...], preferred_element_type=F32).T
    return b[:H] + b[H : 2 * H]


def bias_kernel(z_ref, weight_ref, bias_ref, w_s):
    @pl.when(pl.program_id(0) == 0)
    def _():
        prepare_bias(weight_ref, w_s)

    b = project_bias(z_ref[...].reshape(2 * N, C), w_s)
    for row in range(2):
        store_bias(bias_ref, row, b[:, row * N : (row + 1) * N])


def store_bias(bias_ref, row, b):
    for block in range(N // 128):
        at = (row * (N // 128) + block) * H
        bias_ref[at : at + H, :] = b[:, block * 128 : (block + 1) * 128]


def bias_call(z, bias_weight):
    rows = z.shape[0]
    return pl.pallas_call(
        bias_kernel,
        grid=(rows // 2,),
        in_specs=[
            pl.BlockSpec((2, N, C), lambda r: (r, 0, 0)),
            pl.BlockSpec((H, C), lambda r: (0, 0)),
        ],
        out_specs=pl.BlockSpec((48, 128), lambda r: (r, 0)),
        out_shape=jax.ShapeDtypeStruct((rows * 24, 128), F32),
        scratch_shapes=[pltpu.VMEM((2 * C, C), BF)],
        compiler_params=pltpu.CompilerParams(vmem_limit_bytes=56 * 2**20),
        cost_estimate=pl.CostEstimate(flops=rows * N * C * 20, bytes_accessed=rows * N * C * 4, transcendentals=0),
        name="bias",
    )(z, bias_weight.T)


def project_kernel(carried, valid_ref, z_ref, p_ref, *refs):
    q_ref, k_ref, v_ref, g_ref, w_ref, wg_ref = refs[carried:]
    lane = lax.broadcasted_iota(jnp.int32, (1, C), 1)
    group = lane // D

    @pl.when(pl.program_id(0) == 0)
    def _():
        group_c = lax.broadcasted_iota(jnp.int32, (C, C), 1) // D
        for part in range(3):
            base = p_ref[part]
            if part == 0:
                base = base * (LOG2E * D**-0.5)
            turned = [base] + [pltpu.roll(base, D * m, 1) for m in range(1, 4)]
            for head in range(H):
                block = turned[(0 - head) % H]
                for g in range(1, H):
                    block = jnp.where(group_c == g, turned[(g - head) % H], block)
                high, low = halves(block)
                at = pl.ds((part * H + head) * C, C)
                w_ref[0, :C, at] = high
                w_ref[0, C:, at] = high
                w_ref[1, :C, at] = low
                w_ref[1, C:, at] = low
        high, low = halves(p_ref[3])
        wg_ref[0, :C] = high
        wg_ref[0, C:] = high
        wg_ref[1, :C] = low
        wg_ref[1, C:] = low

    u = normalise(z_ref[0])
    u_high, u_low = halves(u)
    u2 = jnp.concatenate([u_high, u_low], axis=1)

    def project(w):
        return jnp.dot(u2, w[0], preferred_element_type=F32) + jnp.dot(
            u2, w[1], preferred_element_type=F32
        )

    dead = lax.broadcasted_iota(jnp.int32, (N, 1), 0) >= valid_ref[0]
    dead_value = jnp.where(dead, -1e9, 0.0)
    for part in range(3):
        for head in range(H):
            at = pl.ds((part * H + head) * C, C)
            x = project((w_ref[0, :, at], w_ref[1, :, at]))
            high = x.astype(BF).astype(F32)
            low = x - high
            if part == 0:
                out = jnp.where(group == 1, low, high)
                out = jnp.where(group == 3, jnp.where(lane == 3 * D, 1.0, 0.0), out)
                q_ref[0, head] = out.astype(BF)
            elif part == 1:
                out = jnp.where(group == 2, low, high)
                out = jnp.where(group == 3, jnp.where(lane == 3 * D, dead_value, 0.0), out)
                k_ref[0, head] = out.astype(BF)
            else:
                out = jnp.where(group == (head + 1) % H, low, high)
                out = jnp.where(group == (head + 2) % H, 1.0, out)
                out = jnp.where(group == (head + 3) % H, 0.0, out)
                v_ref[0, head] = out.astype(BF)
    g_ref[0] = jax.nn.sigmoid(project((wg_ref[0], wg_ref[1])))


def project_call(z, projection, valid_count, first, count, carry):
    rows = z.shape[0]
    heads = jax.ShapeDtypeStruct((rows, H, N, C), BF)
    head_spec = pl.BlockSpec((1, H, N, C), lambda r, s: (r + first, 0, 0, 0))
    row_spec = pl.BlockSpec((1, N, C), lambda r, s: (r + first, 0, 0))
    carry = carry or []
    return pl.pallas_call(
        functools.partial(project_kernel, len(carry)),
        grid_spec=pltpu.PrefetchScalarGridSpec(
            num_scalar_prefetch=1,
            grid=(count,),
            in_specs=[row_spec, pl.BlockSpec((4, C, C), lambda r, s: (0, 0, 0))]
            + [pl.BlockSpec(memory_space=pl.ANY)] * len(carry),
            out_specs=[head_spec, head_spec, head_spec, row_spec],
            scratch_shapes=[
                pltpu.VMEM((2, 2 * C, 3 * H * C), BF),
                pltpu.VMEM((2, 2 * C, C), BF),
            ],
        ),
        out_shape=[heads, heads, heads, jax.ShapeDtypeStruct((rows, N, C), F32)],
        input_output_aliases={3 + n: n for n in range(len(carry))},
        compiler_params=pltpu.CompilerParams(vmem_limit_bytes=56 * 2**20),
        cost_estimate=pl.CostEstimate(
            flops=count * N * 2 * C * 2 * 13 * C * 8, bytes_accessed=count * N * C * 4 * 8, transcendentals=0
        ),
        name="project",
    )(valid_count, z, projection, *carry)


def project_all(z, projection, valid_count, parts):
    carry = None
    size = z.shape[0] // parts
    for part in range(parts):
        carry = project_call(z, projection, valid_count, part * size, size, carry)
    return carry


def attend_kernel(rows, KT, transposed, with_bias, valid_ref, q_ref, k_ref, v_ref, g_ref, z_ref, o_ref, bias_ref,
                  *refs):
    if with_bias:
        weight_ref, out_ref, local_ref, bias_s, acc_s, o_s, w_s, b_s = refs
    else:
        out_ref, bias_s, acc_s, o_s = refs
    group = lax.broadcasted_iota(jnp.int32, (1, C), 1) // D
    step = pl.program_id(0)
    per = N // 128 * H

    @pl.when(step == 0)
    def _():
        high, low = halves(o_ref[...])
        o_s[0, :C] = high
        o_s[0, C:] = high
        o_s[1, :C] = low
        o_s[1, C:] = low
        if with_bias:
            prepare_bias(weight_ref, w_s)

    @pl.when(step == 0)
    def _():
        for head in range(H):
            for block in range(N // 128):
                at = pl.ds(block * 128, 128)
                if transposed:
                    for part in range(N // 128):
                        tile = bias_ref[pl.ds(block * 128 * per + part * H + head, 128, stride=per), :]
                        bias_s[head, pl.ds(part * 128, 128), at] = tile.T
                else:
                    bias_s[head, :, at] = bias_ref[pl.ds(block * H + head, N, stride=per), :]

    def attend(head, keys):
        q = q_ref[0, head]
        acc = None
        for at in range(0, keys, KT):
            size = min(KT, keys - at)
            s = lax.dot_general(
                q, k_ref[0, head, at : at + size, :], (((1,), (1,)), ((), ())),
                preferred_element_type=F32,
            )
            w = jnp.exp2(s + bias_s[head, :, at : at + size])
            high, low = halves(w)
            v = v_ref[0, head, at : at + size, :]
            term = jnp.dot(high, v, preferred_element_type=F32) + jnp.dot(
                low, v, preferred_element_type=F32
            )
            acc = term if acc is None else acc + term
        acc_s[step % 2, head] = acc

    def finish():
        row = jnp.maximum(step - 1, 0)
        value = low_value = total = None
        for head in range(H):
            acc = acc_s[(step + 1) % 2, head]
            if head == 0:
                value = low_value = total = acc
            else:
                value = jnp.where(group == head, acc, value)
                low_value = jnp.where(group == (head + 1) % H, acc, low_value)
                total = jnp.where(group == (head + 2) % H, acc, total)
        value = value + pltpu.roll(low_value, 3 * D, 1)
        mixed = value / pltpu.roll(total, 2 * D, 1) * g_ref[0]
        high, low = halves(mixed)
        both = jnp.concatenate([high, low], axis=1)
        updated = (
            z_ref[0]
            + jnp.dot(both, o_s[0], preferred_element_type=F32)
            + jnp.dot(both, o_s[1], preferred_element_type=F32)
        )
        out_ref[0] = updated
        if with_bias:
            b_s[row, :H] = project_bias(updated, w_s)

    count = (valid_ref[0] + 127) // 128
    for blocks in range(3, N // 128 + 1):

        @pl.when((count == blocks) & (step < rows))
        def _():
            finish()
            for head in range(H):
                attend(head, blocks * 128)

    @pl.when(step == rows)
    def _():
        finish()
        if with_bias:
            for row in range(rows):
                store_bias(local_ref, row, b_s[row, :H])


def attend_call(q, k, v, g, z, bias, out_weight, valid_count, next_bias=None, KT=256, transposed=False):
    rows = z.shape[0]

    def now(t):
        return jnp.minimum(t, rows - 1)

    def last(t):
        return jnp.maximum(t - 1, 0)

    key_spec = pl.BlockSpec((1, H, N, C), lambda t, s: (now(t), 0, 0, 0))
    row_spec = pl.BlockSpec((1, N, C), lambda t, s: (last(t), 0, 0))
    in_specs = [
        key_spec,
        key_spec,
        key_spec,
        row_spec,
        row_spec,
        pl.BlockSpec((C, C), lambda t, s: (0, 0)),
        pl.BlockSpec((N * N // 128 * H, 128), lambda t, s: (0, 0), pipeline_mode=pl.Buffered(1)),
    ]
    out_specs = [row_spec]
    out_shape = [jax.ShapeDtypeStruct(z.shape, F32)]
    scratch = [
        pltpu.VMEM((H, N, N), F32),
        pltpu.VMEM((2, H, N, C), F32),
        pltpu.VMEM((2, 2 * C, C), BF),
    ]
    args = [q, k, v, g, z, out_weight, bias]
    if next_bias is not None:
        in_specs.append(pl.BlockSpec((H, C), lambda t, s: (0, 0)))
        args.append(next_bias.T)
        out_specs.append(pl.BlockSpec((rows * 24, 128), lambda t, s: (0, 0)))
        out_shape.append(jax.ShapeDtypeStruct((rows * 24, 128), F32))
        scratch += [pltpu.VMEM((2 * C, C), BF), pltpu.VMEM((rows, 8, N), F32)]
    return pl.pallas_call(
        functools.partial(attend_kernel, rows, KT, transposed, next_bias is not None),
        grid_spec=pltpu.PrefetchScalarGridSpec(
            num_scalar_prefetch=1,
            grid=(rows + 1,),
            in_specs=in_specs,
            out_specs=out_specs,
            scratch_shapes=scratch,
        ),
        out_shape=out_shape,
        compiler_params=pltpu.CompilerParams(vmem_limit_bytes=56 * 2**20),
        cost_estimate=pl.CostEstimate(
            flops=rows * N * N * H * 64 * 4, bytes_accessed=rows * N * C * 4 * 8, transcendentals=0
        ),
        name="attend",
    )(valid_count, *args)


def exchange(rows):
    mine, length, width = rows.shape
    parts = length // mine
    sent = rows.reshape(mine, parts, mine, width).transpose(1, 2, 0, 3).reshape(parts, -1, 4, width)
    got = lax.all_to_all(sent, AXES, split_axis=0, concat_axis=0, tiled=True)
    return got.reshape(parts, mine, mine, width).transpose(1, 0, 2, 3).reshape(mine, length, width)


def per_device(
    pair_rows, valid_count, start_proj, start_out, start_bias, end_proj, end_out, end_bias
):
    def gather(local):
        return lax.all_gather(local, AXES, axis=0, tiled=True)

    start_gathered = gather(bias_call(pair_rows, start_bias))
    q, k, v, g = project_all(pair_rows, start_proj, valid_count, 1)
    updated = attend_call(q, k, v, g, pair_rows, start_gathered, start_out, valid_count)[0]
    end_gathered = gather(bias_call(updated, end_bias))
    turned = exchange(updated)
    q, k, v, g = project_all(turned, end_proj, valid_count, 1)
    return attend_call(q, k, v, g, turned, end_gathered, end_out, valid_count, transposed=True)[0]


def solution(mesh):
    return jax.shard_map(
        per_device,
        mesh=mesh,
        in_specs=(P(AXES, None, None), P(), P(), P(), P(), P(), P(), P()),
        out_specs=P(AXES, None, None),
        check_vma=False,
    )
```

```python
import functools
import jax
import jax.numpy as jnp
from jax import lax
from jax.sharding import PartitionSpec as P
from jax.experimental import pallas as pl
from jax.experimental.pallas import tpu as pltpu

LOG2E = 1.4426950408889634
BF = jnp.bfloat16
F32 = jnp.float32
HIGHEST = lax.Precision.HIGHEST
AXES = ("row", "col")
ROWS, N, C, H, D = 6, 768, 128, 4, 32


def normalise(values):
    average = jnp.mean(values, axis=-1, keepdims=True)
    centred = values - average
    variance = jnp.mean(centred * centred, axis=-1, keepdims=True)
    return centred * lax.rsqrt(variance + 1e-05)


def halves(values):
    high = values.astype(BF)
    return high, (values - high.astype(F32)).astype(BF)


def prepare_bias(weight_ref, w_s):
    weight = weight_ref[...] * LOG2E
    high = weight.astype(BF).astype(F32)
    padded = jnp.concatenate([high, weight - high, jnp.zeros((16 - 2 * H, C), F32)], axis=0).astype(BF)
    w_s[...] = jnp.concatenate([padded, padded], axis=1)


def project_bias(values, w_s):
    both = jnp.concatenate(halves(normalise(values)), axis=1)
    b = lax.dot_general(w_s[...], both, (((1,), (1,)), ((), ())), preferred_element_type=F32)
    return b[:H] + b[H : 2 * H]


def bias_kernel(z_ref, weight_ref, bias_ref, w_s):
    @pl.when(pl.program_id(0) == 0)
    def _():
        prepare_bias(weight_ref, w_s)

    b = project_bias(z_ref[...].reshape(2 * N, C), w_s)
    for row in range(2):
        store_bias(bias_ref, row, b[:, row * N : (row + 1) * N])


def store_bias(bias_ref, row, b):
    for block in range(N // 128):
        at = (row * (N // 128) + block) * H
        bias_ref[at : at + H, :] = b[:, block * 128 : (block + 1) * 128]


def bias_call(z, bias_weight):
    rows = z.shape[0]
    return pl.pallas_call(
        bias_kernel,
        grid=(rows // 2,),
        in_specs=[
            pl.BlockSpec((2, N, C), lambda r: (r, 0, 0)),
            pl.BlockSpec((H, C), lambda r: (0, 0)),
        ],
        out_specs=pl.BlockSpec((48, 128), lambda r: (r, 0)),
        out_shape=jax.ShapeDtypeStruct((rows * 24, 128), F32),
        scratch_shapes=[pltpu.VMEM((16, 2 * C), BF)],
        compiler_params=pltpu.CompilerParams(vmem_limit_bytes=56 * 2**20),
        cost_estimate=pl.CostEstimate(flops=rows * N * C * 20, bytes_accessed=rows * N * C * 4, transcendentals=0),
        name="bias",
    )(z, bias_weight.T)


def project_kernel(carried, valid_ref, z_ref, p_ref, *refs):
    q_ref, k_ref, v_ref, g_ref, w_ref, wg_ref = refs[carried:]
    lane = lax.broadcasted_iota(jnp.int32, (1, C), 1)
    group = lane // D

    @pl.when(pl.program_id(0) == 0)
    def _():
        group_c = lax.broadcasted_iota(jnp.int32, (C, C), 1) // D
        for part in range(3):
            base = p_ref[part]
            if part == 0:
                base = base * (LOG2E * D**-0.5)
            turned = [base] + [pltpu.roll(base, D * m, 1) for m in range(1, 4)]
            for head in range(H):
                block = turned[(0 - head) % H]
                for g in range(1, H):
                    block = jnp.where(group_c == g, turned[(g - head) % H], block)
                high, low = halves(block)
                at = pl.ds((part * H + head) * C, C)
                w_ref[0, :C, at] = high
                w_ref[0, C:, at] = high
                w_ref[1, :C, at] = low
                w_ref[1, C:, at] = low
        high, low = halves(p_ref[3])
        wg_ref[0, :C] = high
        wg_ref[0, C:] = high
        wg_ref[1, :C] = low
        wg_ref[1, C:] = low

    u = normalise(z_ref[0])
    u_high, u_low = halves(u)
    u2 = jnp.concatenate([u_high, u_low], axis=1)

    def project(w):
        return jnp.dot(u2, w[0], preferred_element_type=F32) + jnp.dot(
            u2, w[1], preferred_element_type=F32
        )

    dead = lax.broadcasted_iota(jnp.int32, (N, 1), 0) >= valid_ref[0]
    dead_value = jnp.where(dead, -1e9, 0.0)
    for part in range(3):
        for head in range(H):
            at = pl.ds((part * H + head) * C, C)
            x = project((w_ref[0, :, at], w_ref[1, :, at]))
            high = x.astype(BF).astype(F32)
            low = x - high
            if part == 0:
                out = jnp.where(group == 1, low, high)
                out = jnp.where(group == 3, jnp.where(lane == 3 * D, 1.0, 0.0), out)
                q_ref[0, head] = out.astype(BF)
            elif part == 1:
                out = jnp.where(group == 2, low, high)
                out = jnp.where(group == 3, jnp.where(lane == 3 * D, dead_value, 0.0), out)
                k_ref[0, head] = out.astype(BF)
            else:
                out = jnp.where(group == (head + 1) % H, low, high)
                out = jnp.where(group == (head + 2) % H, 1.0, out)
                out = jnp.where(group == (head + 3) % H, 0.0, out)
                v_ref[0, head] = out.astype(BF)
    g_ref[0] = jax.nn.sigmoid(project((wg_ref[0], wg_ref[1])))


def project_call(z, projection, valid_count, first, count, carry):
    rows = z.shape[0]
    heads = jax.ShapeDtypeStruct((rows, H, N, C), BF)
    head_spec = pl.BlockSpec((1, H, N, C), lambda r, s: (r + first, 0, 0, 0))
    row_spec = pl.BlockSpec((1, N, C), lambda r, s: (r + first, 0, 0))
    carry = carry or []
    return pl.pallas_call(
        functools.partial(project_kernel, len(carry)),
        grid_spec=pltpu.PrefetchScalarGridSpec(
            num_scalar_prefetch=1,
            grid=(count,),
            in_specs=[row_spec, pl.BlockSpec((4, C, C), lambda r, s: (0, 0, 0))]
            + [pl.BlockSpec(memory_space=pl.ANY)] * len(carry),
            out_specs=[head_spec, head_spec, head_spec, row_spec],
            scratch_shapes=[
                pltpu.VMEM((2, 2 * C, 3 * H * C), BF),
                pltpu.VMEM((2, 2 * C, C), BF),
            ],
        ),
        out_shape=[heads, heads, heads, jax.ShapeDtypeStruct((rows, N, C), F32)],
        input_output_aliases={3 + n: n for n in range(len(carry))},
        compiler_params=pltpu.CompilerParams(vmem_limit_bytes=56 * 2**20),
        cost_estimate=pl.CostEstimate(
            flops=count * N * 2 * C * 2 * 13 * C * 8, bytes_accessed=count * N * C * 4 * 8, transcendentals=0
        ),
        name="project",
    )(valid_count, z, projection, *carry)


def project_all(z, projection, valid_count, parts):
    carry = None
    size = z.shape[0] // parts
    for part in range(parts):
        carry = project_call(z, projection, valid_count, part * size, size, carry)
    return carry


def attend_kernel(rows, KT, transposed, with_bias, valid_ref, q_ref, k_ref, v_ref, g_ref, z_ref, o_ref, bias_ref,
                  *refs):
    if with_bias:
        weight_ref, out_ref, local_ref, bias_s, acc_s, o_s, w_s, b_s = refs
    else:
        out_ref, bias_s, acc_s, o_s = refs
    group = lax.broadcasted_iota(jnp.int32, (1, C), 1) // D
    step = pl.program_id(0)
    per = N // 128 * H

    @pl.when(step == 0)
    def _():
        high, low = halves(o_ref[...])
        o_s[0, :C] = high
        o_s[0, C:] = high
        o_s[1, :C] = low
        o_s[1, C:] = low
        if with_bias:
            prepare_bias(weight_ref, w_s)

    def arrange(block):
        at = pl.ds(block * 128, 128)
        for head in range(H):
            if transposed:
                for part in range(N // 128):
                    tile = bias_ref[pl.ds(block * 128 * per + part * H + head, 128, stride=per), :]
                    bias_s[head, pl.ds(part * 128, 128), at] = tile.T
            else:
                bias_s[head, :, at] = bias_ref[pl.ds(block * H + head, N, stride=per), :]

    for block in range(N // 128):

        @pl.when((step == 0) & (block * 128 < valid_ref[0]))
        def _():
            arrange(block)

    def attend(head, keys):
        q = q_ref[0, head]
        acc = None
        for at in range(0, keys, KT):
            size = min(KT, keys - at)
            s = lax.dot_general(
                q, k_ref[0, head, at : at + size, :], (((1,), (1,)), ((), ())),
                preferred_element_type=F32,
            )
            w = jnp.exp2(s + bias_s[head, :, at : at + size])
            high, low = halves(w)
            v = v_ref[0, head, at : at + size, :]
            term = jnp.dot(high, v, preferred_element_type=F32) + jnp.dot(
                low, v, preferred_element_type=F32
            )
            acc = term if acc is None else acc + term
        acc_s[step % 2, head] = acc

    def finish():
        row = jnp.maximum(step - 1, 0)
        value = low_value = total = None
        for head in range(H):
            acc = acc_s[(step + 1) % 2, head]
            if head == 0:
                value = low_value = total = acc
            else:
                value = jnp.where(group == head, acc, value)
                low_value = jnp.where(group == (head + 1) % H, acc, low_value)
                total = jnp.where(group == (head + 2) % H, acc, total)
        value = value + pltpu.roll(low_value, 3 * D, 1)
        mixed = value / pltpu.roll(total, 2 * D, 1) * g_ref[0]
        high, low = halves(mixed)
        both = jnp.concatenate([high, low], axis=1)
        updated = (
            z_ref[0]
            + jnp.dot(both, o_s[0], preferred_element_type=F32)
            + jnp.dot(both, o_s[1], preferred_element_type=F32)
        )
        out_ref[0] = updated
        if with_bias:
            b_s[row, :H] = project_bias(updated, w_s)

    count = (valid_ref[0] + 127) // 128
    for blocks in range(3, N // 128 + 1):

        @pl.when((count == blocks) & (step < rows))
        def _():
            finish()
            for head in range(H):
                attend(head, blocks * 128)

    @pl.when(step == rows)
    def _():
        finish()
        if with_bias:
            for row in range(rows):
                store_bias(local_ref, row, b_s[row, :H])


def attend_call(q, k, v, g, z, bias, out_weight, valid_count, next_bias=None, KT=256, transposed=False):
    rows = z.shape[0]

    def now(t):
        return jnp.minimum(t, rows - 1)

    def last(t):
        return jnp.maximum(t - 1, 0)

    key_spec = pl.BlockSpec((1, H, N, C), lambda t, s: (now(t), 0, 0, 0))
    row_spec = pl.BlockSpec((1, N, C), lambda t, s: (last(t), 0, 0))
    in_specs = [
        key_spec,
        key_spec,
        key_spec,
        row_spec,
        row_spec,
        pl.BlockSpec((C, C), lambda t, s: (0, 0)),
        pl.BlockSpec((N * N // 128 * H, 128), lambda t, s: (0, 0), pipeline_mode=pl.Buffered(1)),
    ]
    out_specs = [row_spec]
    out_shape = [jax.ShapeDtypeStruct(z.shape, F32)]
    scratch = [
        pltpu.VMEM((H, N, N), F32),
        pltpu.VMEM((2, H, N, C), F32),
        pltpu.VMEM((2, 2 * C, C), BF),
    ]
    args = [q, k, v, g, z, out_weight, bias]
    if next_bias is not None:
        in_specs.append(pl.BlockSpec((H, C), lambda t, s: (0, 0)))
        args.append(next_bias.T)
        out_specs.append(pl.BlockSpec((rows * 24, 128), lambda t, s: (0, 0)))
        out_shape.append(jax.ShapeDtypeStruct((rows * 24, 128), F32))
        scratch += [pltpu.VMEM((2 * C, C), BF), pltpu.VMEM((rows, 8, N), F32)]
    return pl.pallas_call(
        functools.partial(attend_kernel, rows, KT, transposed, next_bias is not None),
        grid_spec=pltpu.PrefetchScalarGridSpec(
            num_scalar_prefetch=1,
            grid=(rows + 1,),
            in_specs=in_specs,
            out_specs=out_specs,
            scratch_shapes=scratch,
        ),
        out_shape=out_shape,
        compiler_params=pltpu.CompilerParams(vmem_limit_bytes=56 * 2**20),
        cost_estimate=pl.CostEstimate(
            flops=rows * N * N * H * 64 * 4, bytes_accessed=rows * N * C * 4 * 8, transcendentals=0
        ),
        name="attend",
    )(valid_count, *args)


def exchange(rows):
    mine, length, width = rows.shape
    parts = length // mine
    sent = rows.reshape(mine, parts, mine, width).transpose(1, 2, 0, 3).reshape(parts, -1, 4, width)
    got = lax.all_to_all(sent, AXES, split_axis=0, concat_axis=0, tiled=True)
    return got.reshape(parts, mine, mine, width).transpose(1, 0, 2, 3).reshape(mine, length, width)


def per_device(
    pair_rows, valid_count, start_proj, start_out, start_bias, end_proj, end_out, end_bias
):
    def gather(local):
        return lax.all_gather(local, AXES, axis=0, tiled=True)

    start_gathered = gather(bias_call(pair_rows, start_bias))
    q, k, v, g = project_all(pair_rows, start_proj, valid_count, 1)
    updated = attend_call(q, k, v, g, pair_rows, start_gathered, start_out, valid_count)[0]
    end_gathered = gather(bias_call(updated, end_bias))
    turned = exchange(updated)
    q, k, v, g = project_all(turned, end_proj, valid_count, 1)
    return attend_call(q, k, v, g, turned, end_gathered, end_out, valid_count, transposed=True)[0]


def solution(mesh):
    return jax.shard_map(
        per_device,
        mesh=mesh,
        in_specs=(P(AXES, None, None), P(), P(), P(), P(), P(), P(), P()),
        out_specs=P(AXES, None, None),
        check_vma=False,
    )
```
